32 devices in a mesh: parts: 2 (over y), wide: 4 (over z), rep: 2 (over x), sub: 2 (over core).
Axes of the slice: x: 2, y: 2, z: 4, core: 2. Of those that a mesh axis runs over, the one named last changes fastest.
Arguments:
- activations: bfloat16 [8, 2048, 512], P(('parts', 'wide'), 'sub'), parts along dimension 0, may hold values from -6 to 6
- deltas: bfloat16 [8, 2048, 512], P(('parts', 'wide'), 'sub'), parts along dimension 0, may hold values from -6 to 6
- act_factor: bfloat16 [512, 512], P(None, 'rep'), as said below
- delta_factor: bfloat16 [512, 512], P(None, 'rep'), as said below
- queries: bfloat16 [1280, 512, 512], P(None, ('rep', 'wide'), 'sub'), may hold values from -0.00059890747 to 0.00059890747
- assignment: int32 [8], P('parts'), parts along dimension 0, may hold values from 0 to 3, each once
- padding: int32 [8], P(('parts', 'wide')), parts along dimension 0, may hold values from 0 to 1023
Outputs:
- scores: float32 [8, 1280], P(('parts', 'wide'), ('rep', 'sub')), parts along dimension 0
The draws below stay inside these ranges and needn't reach their ends.
There are 2 independent parts, one for each index of `parts`. The reference program is written for one: setup_inputs(seed, part) draws one part's arguments, and reference() takes and returns one part's arrays. A program takes and returns all parts, laid end to end along the dimension named above; an argument that names none is the same for every part. Nothing has to cross between parts.
Inputs may be any that keep to these rules, and one draw needn't show every extreme that they name: `act_factor`: symmetric and positive definite. `delta_factor`: symmetric and positive definite. `assignment`: each number once.
All inputs are finite; a program needn't handle non-finite values.
Results may differ from the reference program's by a relative error of at most 0.005.
Values may be sent and summed in bfloat16 or wider, within the bound.
No kernel may reach another device: no remote copies, remote signals or barrier semaphores. Data moves between devices by JAX's collectives and lax.ppermute only.
A program may use at most 128 MiB of HBM per device.

```python
import jax
import jax.numpy as jnp
from jax import lax

PROJ = 512
SEQ_LEN = 2048
QUERIES = 1280
SEQS = 4


def make_factor(key):
    first, second = jax.random.split(key)
    diag_part = jnp.exp(jax.random.uniform(first, (PROJ,), jnp.float32, jnp.log(0.5), jnp.log(2.0)))
    noise = jax.random.normal(second, (PROJ, PROJ), jnp.float32)
    symmetric = (noise + noise.T) * (0.2 / (2.0 * PROJ) ** 0.5)
    return (jnp.diag(diag_part) + symmetric).astype(jnp.bfloat16)


def draw_act_factor(key, part):
    return make_factor(jax.random.fold_in(key, 11))


def draw_delta_factor(key, part):
    return make_factor(jax.random.fold_in(key, 23))


def set_ends(values, rng, smallest, high):
    index_at = [jax.random.randint(jax.random.fold_in(rng, axis), (), 0, length) for axis, length in enumerate(values.shape)]
    longest = values.shape.index(max(values.shape))
    next_to = index_at[:longest] + [(index_at[longest] + 1) % values.shape[longest]] + index_at[longest + 1:]
    return values.at[tuple(index_at)].set(smallest).at[tuple(next_to)].set(high)


def with_spikes(entries, key, source, target, parts, factor):
    def block_of(dim):
        return (jnp.arange(entries.shape[dim]) // (entries.shape[dim] // parts)).reshape((-1,) + (1,) * (entries.ndim - 1 - dim))

    one_side = jax.random.permutation(key, parts)[block_of(target)]
    other_side = (block_of(target) + parts // 2) % parts
    return jnp.where((block_of(source) == one_side) | (block_of(source) == other_side), factor * entries, entries)


def level_of(stream_key, extent, shards, smallest, high):
    factor_of = 1.0
    for axis_at, shards_of in shards:
        draws = jax.random.uniform(jax.random.fold_in(jax.random.fold_in(stream_key, 6), axis_at), (shards_of,), jnp.float32, smallest / len(shards), high / len(shards))
        factor_of = factor_of * jnp.repeat(jnp.exp(draws), extent[axis_at] // shards_of).reshape((-1,) + (1,) * (len(extent) - 1 - axis_at))
    return factor_of


def scatter_about(key, extent, deviation, most, cuts=(), kind=jnp.bfloat16):
    result = deviation * jax.random.normal(key, extent, jnp.float32)
    if cuts:
        result = result * level_of(key, extent, cuts, -0.22, 0.18)
    return jnp.clip(result, -most, most).astype(kind)


def heavy_noise(rng, extent, deviation, reach, shards, heavy, dtype=jnp.bfloat16):
    drawn = deviation * jax.random.normal(rng, extent, jnp.float32)
    if shards:
        drawn = drawn * level_of(rng, extent, shards, -0.22, 0.18)
    return jnp.clip(with_spikes(drawn, jax.random.fold_in(rng, 3), *heavy), -reach, reach).astype(dtype)


def setup_inputs(seed: int = 0, part: int = 0) -> dict:
    seeds = jax.random.split(jax.random.key(seed), 8)
    own_keys = jax.random.split(jax.random.fold_in(seeds[7], part), 8)
    return {
        "activations": scatter_about(own_keys[0], (SEQS, SEQ_LEN, PROJ), 1.0, 6.0, ((0, 4), (1, 2))),
        "deltas": scatter_about(own_keys[1], (SEQS, SEQ_LEN, PROJ), 1.0, 6.0, ((0, 4), (1, 2))),
        "act_factor": draw_act_factor(jax.random.fold_in(seeds[7], 71), part),
        "delta_factor": draw_delta_factor(jax.random.fold_in(seeds[7], 71), part),
        "queries": heavy_noise(seeds[4], (QUERIES, PROJ, PROJ), 0.0001, 0.00059890747, ((1, 8), (2, 2)), (1, 0, 8, 2.0)),
        "assignment": jax.random.permutation(own_keys[5], SEQS).astype(jnp.int32),
        "padding": set_ends(jax.random.randint(own_keys[6], (SEQS,), 0, SEQ_LEN // 2), jax.random.fold_in(own_keys[6], 1), 0, (SEQ_LEN // 2) - 1).astype(jnp.int32),
    }


def reference(activations, deltas, act_factor, delta_factor, queries, assignment, padding):
    positions = lax.broadcasted_iota(jnp.int32, (SEQS, SEQ_LEN), 1)
    kept_mask = positions < (SEQ_LEN - padding)[:, None]
    masked = jnp.where(kept_mask[:, :, None], deltas, jnp.zeros((), jnp.bfloat16))
    delta_proj = jnp.dot(masked.reshape(SEQS * SEQ_LEN, PROJ), delta_factor, preferred_element_type=jnp.float32)
    delta_proj = delta_proj.astype(jnp.bfloat16).reshape(SEQS, SEQ_LEN, PROJ)
    act_proj = jnp.dot(activations.reshape(SEQS * SEQ_LEN, PROJ), act_factor, preferred_element_type=jnp.float32)
    act_proj = act_proj.astype(jnp.bfloat16).reshape(SEQS, SEQ_LEN, PROJ)
    grad = jnp.einsum("nti,ntj->nij", delta_proj.astype(jnp.float32), act_proj.astype(jnp.float32))
    grad = grad.astype(jnp.bfloat16)
    raw = jnp.dot(grad.reshape(SEQS, PROJ * PROJ), queries.reshape(QUERIES, PROJ * PROJ).T, preferred_element_type=jnp.float32)
    scores = jnp.zeros((SEQS, QUERIES), jnp.float32).at[assignment].set(raw)
    return scores
```

```python
import functools

import jax
import jax.numpy as jnp
from jax import lax
from jax.experimental import pallas as pl
from jax.experimental.pallas import tpu as pltpu
from jax.sharding import PartitionSpec as P

GROUP = 16
F32 = jnp.float32
BF16 = jnp.bfloat16
NT = (((1,), (1,)), ((), ()))
TN = (((0,), (0,)), ((), ()))


def row_product_kernel(token_steps, pad_ref, deltas_ref, acts_ref, factor_ref, out_ref):
    step = pl.program_id(0)
    tokens = deltas_ref.shape[0]
    first = (lax.axis_index("sub") * token_steps + step) * tokens
    limit = lax.axis_size("sub") * token_steps * tokens - pad_ref[0]
    position = first + lax.broadcasted_iota(jnp.int32, (tokens, 1), 0)
    masked = jnp.where(position < limit, deltas_ref[...], jnp.zeros((), BF16))
    proj = jnp.dot(masked, factor_ref[...], preferred_element_type=F32).astype(BF16)
    term = lax.dot_general(proj, acts_ref[...], TN, preferred_element_type=F32)

    @pl.when(step == 0)
    def _():
        out_ref[...] = term

    @pl.when(step > 0)
    def _():
        out_ref[...] += term


def row_product(padding, deltas, acts, factor):
    tokens, width = deltas.shape
    rows = factor.shape[1]
    steps = 4 if tokens % 1024 == 0 else 1
    block = tokens // steps
    return pl.pallas_call(
        functools.partial(row_product_kernel, steps),
        grid=(steps,),
        out_shape=jax.ShapeDtypeStruct((rows, width), F32),
        in_specs=[
            pl.BlockSpec(memory_space=pltpu.SMEM),
            pl.BlockSpec((block, width), lambda i: (i, 0)),
            pl.BlockSpec((block, width), lambda i: (i, 0)),
            pl.BlockSpec((width, rows), lambda i: (0, 0)),
        ],
        out_specs=pl.BlockSpec((rows, width), lambda i: (0, 0)),
        compiler_params=pltpu.CompilerParams(vmem_limit_bytes=12 << 20),
        cost_estimate=pl.CostEstimate(
            flops=4 * tokens * width * rows, bytes_accessed=4 * tokens * width, transcendentals=0
        ),
    )(padding, deltas, acts, factor)


def grad_kernel(parts, wide, seq_ref, mine_ref, other_ref, factor_ref, far_ref, out_ref):
    rep, sub = lax.axis_index("rep"), lax.axis_index("sub")
    half = factor_ref.shape[1]
    rows = mine_ref.shape[0] // (parts * wide)
    summed = mine_ref[...] + other_ref[...]
    high = summed.astype(BF16)
    low = (summed - high.astype(F32)).astype(BF16)

    def emit(grad):
        tag = lax.broadcasted_iota(jnp.int32, (GROUP, half), 1) == seq_ref[0]
        for part in range(parts):
            for place in range(wide):
                block = part * wide + place
                start = (place * parts + part) * rows
                out_ref[block, :rows, :] = grad[start : start + rows].astype(BF16)
                out_ref[block, rows:, :] = tag.astype(F32).astype(BF16)

    def product(values, near, far, near_rows):
        first, second = values[:, :half], values[:, half:]
        if near_rows == 0:
            a, b = first, second
        else:
            a, b = second, first
        return lax.dot_general(a, near, NT, preferred_element_type=F32) + jnp.dot(
            b, far, preferred_element_type=F32
        )

    @pl.when(rep == sub)
    def _():
        whole = factor_ref[...]
        emit(
            jnp.dot(high, whole, preferred_element_type=F32)
            + jnp.dot(low, whole, preferred_element_type=F32)
        )

    for index in range(2):

        @pl.when((rep != sub) & (rep == index))
        def _():
            other = 1 - index
            near = factor_ref[other * half : (other + 1) * half, :]
            far = far_ref[...]
            emit(product(high, near, far, index) + product(low, near, far, index))


def grad_blocks(parts, wide, seq, mine, other, factor, far):
    rows, width = mine.shape
    block = rows // (parts * wide)
    half = factor.shape[1]
    vmem = pl.BlockSpec(memory_space=pltpu.VMEM)
    return pl.pallas_call(
        functools.partial(grad_kernel, parts, wide),
        out_shape=jax.ShapeDtypeStruct((parts * wide, block + GROUP, half), BF16),
        in_specs=[pl.BlockSpec(memory_space=pltpu.SMEM)] + [vmem] * 4,
        out_specs=vmem,
        compiler_params=pltpu.CompilerParams(vmem_limit_bytes=12 << 20),
        cost_estimate=pl.CostEstimate(
            flops=4 * rows * width * half, bytes_accessed=12 * rows * width, transcendentals=0
        ),
    )(seq, mine, other, factor, far)


def score_kernel(blocks, pieces, grads_ref, queries_ref, out_ref, held, sems):
    seqs, padded, width = grads_ref.shape
    rows = padded - GROUP
    total = queries_ref.shape[0]
    piece = total // pieces
    start = pl.multiple_of(lax.axis_index("parts") * rows, rows)

    def copy(i):
        return pltpu.make_async_copy(
            queries_ref.at[pl.ds(i * piece, piece), pl.ds(start, rows), :],
            held.at[pl.ds(i * piece, piece)],
            sems.at[i],
        )

    for i in range(pieces):
        copy(i).start()

    lanes = seqs * GROUP
    weights = jnp.concatenate(
        [
            grads_ref[:, g : g + GROUP, :].reshape(lanes, width)
            for g in range(0, rows, GROUP)
        ],
        axis=1,
    )
    lane = lax.broadcasted_iota(jnp.int32, (GROUP, lanes), 1)
    diagonal = lax.broadcasted_iota(jnp.int32, (GROUP, lanes), 0) == lane % GROUP
    tags = grads_ref[:, rows, :]
    owner = lax.broadcasted_iota(jnp.int32, (seqs, lanes), 0) == (
        lax.broadcasted_iota(jnp.int32, (seqs, lanes), 1) // GROUP
    )
    place = lax.dot_general(
        tags, owner.astype(F32).astype(BF16), TN, preferred_element_type=F32
    )[:seqs]

    per_block = total // blocks
    sub_pieces = pieces // blocks
    for block in range(blocks):
        sums = []
        for j in range(sub_pieces):
            i = block * sub_pieces + j
            copy(i).wait()
            at = pl.ds(i * piece, piece)
            rows_of = jnp.concatenate(
                [
                    held[at, g : g + GROUP, :].reshape(piece * GROUP, width)
                    for g in range(0, rows, GROUP)
                ],
                axis=1,
            )
            found = lax.dot_general(rows_of, weights, NT, preferred_element_type=F32)
            kept = jnp.where(diagonal, found.reshape(piece, GROUP, lanes), 0.0)
            sums.append(jnp.sum(kept, axis=1))
        by_query = sums[0] if len(sums) == 1 else jnp.concatenate(sums, axis=0)
        scores = lax.dot_general(
            place, by_query, NT, preferred_element_type=F32, precision=lax.Precision.HIGHEST
        )
        for m in range(seqs):
            out_ref[m * blocks + block] = scores[m : m + 1]


def score_blocks(blocks, grads, queries):
    seqs, padded, width = grads.shape
    rows = padded - GROUP
    total = queries.shape[0]
    pieces = blocks * 2
    return pl.pallas_call(
        functools.partial(score_kernel, blocks, pieces),
        out_shape=jax.ShapeDtypeStruct((seqs * blocks, 1, total // blocks), F32),
        in_specs=[pl.BlockSpec(memory_space=pltpu.VMEM), pl.BlockSpec(memory_space=pl.ANY)],
        out_specs=pl.BlockSpec(memory_space=pltpu.VMEM),
        scratch_shapes=[
            pltpu.VMEM((total, rows, width), BF16),
            pltpu.SemaphoreType.DMA((pieces,)),
        ],
        compiler_params=pltpu.CompilerParams(vmem_limit_bytes=48 << 20),
        cost_estimate=pl.CostEstimate(
            flops=2 * total * rows * width * 128,
            bytes_accessed=2 * total * rows * width,
            transcendentals=0,
        ),
    )(grads, queries)


def shared(activations, deltas, act_factor, delta_factor, queries, assignment, padding):
    parts, wide = lax.axis_size("parts"), lax.axis_size("wide")
    rep, sub = lax.axis_size("rep"), lax.axis_size("sub")
    half = act_factor.shape[1]
    own_block = lax.dynamic_slice_in_dim(act_factor, lax.axis_index("rep") * half, half, axis=0)
    far_block = lax.ppermute(own_block, "rep", [(0, 1), (1, 0)])
    mine = row_product(padding, deltas[0], activations[0], delta_factor)
    other = lax.ppermute(mine, "sub", [(0, 1), (1, 0)])
    seq = assignment[lax.axis_index("wide")] + lax.axis_index("parts") * wide
    sent = grad_blocks(parts, wide, seq[None], mine, other, act_factor, far_block)
    grads = lax.all_to_all(sent, ("parts", "wide"), split_axis=0, concat_axis=0, tiled=True)
    partial = score_blocks(rep * sub, grads, queries)
    gathered = lax.all_to_all(
        partial, ("parts", "wide", "rep", "sub"), split_axis=0, concat_axis=0, tiled=True
    )
    return jnp.sum(gathered, axis=0)


def general(activations, deltas, act_factor, delta_factor, queries, assignment, padding):
    seq_dev, tok_dev, _ = activations.shape
    full_length = tok_dev * lax.axis_size("sub")
    token_start = lax.axis_index("sub") * tok_dev
    positions = token_start + lax.broadcasted_iota(jnp.int32, (seq_dev, tok_dev), 1)
    kept_mask = positions < (full_length - padding)[:, None]
    masked = jnp.where(kept_mask[:, :, None], deltas, jnp.zeros((), BF16))
    delta_proj = jnp.einsum(
        "stw,wi->sti", masked, delta_factor, preferred_element_type=F32
    ).astype(BF16)
    act_proj = jnp.einsum(
        "stw,wj->stj",
        activations,
        lax.all_gather(act_factor, "rep", axis=1, tiled=True),
        preferred_element_type=F32,
    ).astype(BF16)
    partial_value = jnp.einsum("sti,stj->sij", delta_proj, act_proj, preferred_element_type=F32)
    summed = lax.psum_scatter(partial_value, "sub", scatter_dimension=2, tiled=True).astype(BF16)
    regrouped = lax.all_to_all(summed, "wide", split_axis=1, concat_axis=0, tiled=True)
    seq_total = regrouped.shape[0]
    grad_rows = regrouped.reshape(seq_total, -1)
    query_rows = queries.reshape(queries.shape[0], -1)
    partial_scores = lax.dot_general(grad_rows, query_rows, NT, preferred_element_type=F32)
    inverse_order = (
        jnp.zeros((seq_total,), jnp.int32)
        .at[assignment]
        .set(jnp.arange(seq_total, dtype=jnp.int32))
    )
    ranked = jnp.take(partial_scores, inverse_order, axis=0)
    by_column = lax.psum_scatter(ranked, ("rep", "sub"), scatter_dimension=1, tiled=True)
    return lax.psum_scatter(by_column, "wide", scatter_dimension=0, tiled=True)


def shards(activations, deltas, act_factor, delta_factor, queries, assignment, padding):
    parts, wide = lax.axis_size("parts"), lax.axis_size("wide")
    rep, sub = lax.axis_size("rep"), lax.axis_size("sub")
    fits = (
        rep == 2
        and sub == 2
        and activations.shape[0] == 1
        and queries.shape[1] % (parts * GROUP) == 0
        and parts * wide * GROUP <= 128
        and queries.shape[0] % (2 * rep * sub) == 0
        and act_factor.shape[1] % 128 == 0
    )
    body = shared if fits else general
    return body(activations, deltas, act_factor, delta_factor, queries, assignment, padding)


def solution(mesh):
    placed = (
        P(("parts", "wide"), "sub", None),
        P(("parts", "wide"), "sub", None),
        P(None, "rep"),
        P(None, "rep"),
        P(None, ("rep", "wide"), "sub"),
        P("parts"),
        P(("parts", "wide")),
    )
    return jax.shard_map(
        shards,
        mesh=mesh,
        in_specs=placed,
        out_specs=P(("parts", "wide"), ("rep", "sub")),
        check_vma=False,
    )
```

```python
import functools

import jax
import jax.numpy as jnp
from jax import lax
from jax.experimental import pallas as pl
from jax.experimental.pallas import tpu as pltpu
from jax.sharding import PartitionSpec as P

GROUP = 16
F32 = jnp.float32
BF16 = jnp.bfloat16
NT = (((1,), (1,)), ((), ()))
TN = (((0,), (0,)), ((), ()))


def row_product_kernel(
    pad_ref, deltas_ref, acts_ref, row_factor_ref, col_factor_ref, queries_ref,
    out_ref, col_out_ref, early_ref,
    pad_in, deltas_in, acts_in, factor_in, sems,
):
    steps, tokens, _ = deltas_in.shape
    first = lax.axis_index("sub") * steps * tokens

    def copy(source, held, which, i):
        return pltpu.make_async_copy(
            source.at[pl.ds(i * tokens, tokens), :], held.at[i], sems.at[which, i]
        )

    row_copy = pltpu.make_async_copy(row_factor_ref, factor_in, sems.at[2, 0])
    col_copy = pltpu.make_async_copy(col_factor_ref, col_out_ref, sems.at[2, 1])
    pad_copy = pltpu.make_async_copy(pad_ref, pad_in, sems.at[2, 2])
    pad_copy.start()
    row_copy.start()
    for i in range(steps):
        copy(deltas_ref, deltas_in, 0, i).start()
        copy(acts_ref, acts_in, 1, i).start()
    col_copy.start()
    early_copy = pltpu.make_async_copy(
        queries_ref.at[pl.ds(0, early_ref.shape[0])], early_ref, sems.at[2, 3]
    )
    early_copy.start()
    out_ref[...] = jnp.zeros(out_ref.shape, F32)
    pad_copy.wait()
    row_copy.wait()
    limit = lax.axis_size("sub") * steps * tokens - pad_in[0]

    def step(i, carry):
        copy(deltas_ref, deltas_in, 0, i).wait()
        copy(acts_ref, acts_in, 1, i).wait()
        position = first + i * tokens + lax.broadcasted_iota(jnp.int32, (tokens, 1), 0)
        masked = jnp.where(position < limit, deltas_in[i], jnp.zeros((), BF16))
        proj = jnp.dot(masked, factor_in[...], preferred_element_type=F32).astype(BF16)
        out_ref[...] += lax.dot_general(proj, acts_in[i], TN, preferred_element_type=F32)
        return carry

    lax.fori_loop(0, steps, step, 0)
    col_copy.wait()
    early_copy.wait()


def row_product(padding, deltas, acts, row_factor, col_factor, queries, early):
    tokens, width = deltas.shape
    rows = row_factor.shape[1]
    steps = max(1, tokens // 512)
    hbm = pl.BlockSpec(memory_space=pltpu.HBM)
    vmem = pl.BlockSpec(memory_space=pltpu.VMEM)
    operands = [padding] + [
        pltpu.with_memory_space_constraint(x, pltpu.HBM)
        for x in (deltas, acts, row_factor, col_factor, queries)
    ]
    return pl.pallas_call(
        row_product_kernel,
        out_shape=(
            jax.ShapeDtypeStruct((rows, width), F32),
            jax.ShapeDtypeStruct(col_factor.shape, BF16),
            pltpu.VMEM((early,) + queries.shape[1:], BF16),
        ),
        in_specs=[pl.BlockSpec(memory_space=pl.ANY)] + [hbm] * 5,
        out_specs=(vmem, vmem, vmem),
        scratch_shapes=[
            pltpu.SMEM(padding.shape, jnp.int32),
            pltpu.VMEM((steps, tokens // steps, width), BF16),
            pltpu.VMEM((steps, tokens // steps, width), BF16),
            pltpu.VMEM(row_factor.shape, BF16),
            pltpu.SemaphoreType.DMA((3, max(4, steps))),
        ],
        compiler_params=pltpu.CompilerParams(vmem_limit_bytes=12 << 20),
        cost_estimate=pl.CostEstimate(
            flops=4 * tokens * width * rows, bytes_accessed=4 * tokens * width, transcendentals=0
        ),
    )(*operands)


def grad_kernel(wide, mine_ref, other_ref, factor_ref, far_ref, *outs_and_scratch):
    *outs, held = outs_and_scratch
    rep, sub, place = (lax.axis_index(a) for a in ("rep", "sub", "wide"))
    half = factor_ref.shape[1]
    rows = mine_ref.shape[0] // wide
    summed = mine_ref[...] + other_ref[...]
    high = summed.astype(BF16)
    low = (summed - high.astype(F32)).astype(BF16)

    @pl.when(rep == sub)
    def _():
        whole = factor_ref[...]
        held[...] = jnp.dot(high, whole, preferred_element_type=F32) + jnp.dot(
            low, whole, preferred_element_type=F32
        )

    for index in range(2):

        @pl.when((rep != sub) & (rep == index))
        def _():
            here = slice(index * half, (index + 1) * half)
            there = slice((1 - index) * half, (2 - index) * half)
            near, far = factor_ref[there, :], far_ref[...]
            held[...] = (
                lax.dot_general(high[:, here], near, NT, preferred_element_type=F32)
                + lax.dot_general(low[:, here], near, NT, preferred_element_type=F32)
                + jnp.dot(high[:, there], far, preferred_element_type=F32)
                + jnp.dot(low[:, there], far, preferred_element_type=F32)
            )

    for k in range(wide):
        start = pl.multiple_of((place ^ k) * rows, rows)
        outs[k][...] = held[pl.ds(start, rows), :].astype(BF16)


def grad_blocks(wide, mine, other, factor, far):
    rows, width = mine.shape
    half = factor.shape[1]
    vmem = pl.BlockSpec(memory_space=pltpu.VMEM)
    return pl.pallas_call(
        functools.partial(grad_kernel, wide),
        out_shape=[jax.ShapeDtypeStruct((rows // wide, half), BF16)] * wide,
        in_specs=[vmem] * 4,
        out_specs=[vmem] * wide,
        scratch_shapes=[pltpu.VMEM((rows, half), F32)],
        compiler_params=pltpu.CompilerParams(vmem_limit_bytes=8 << 20),
        cost_estimate=pl.CostEstimate(
            flops=4 * rows * width * half, bytes_accessed=12 * rows * width, transcendentals=0
        ),
    )(mine, other, factor, far)


def fetch_kernel(first, queries_ref, out_ref, sem):
    copy = pltpu.make_async_copy(queries_ref.at[pl.ds(first, out_ref.shape[0])], out_ref, sem)
    copy.start()
    copy.wait()


def fetch(queries, first, count):
    return pl.pallas_call(
        functools.partial(fetch_kernel, first),
        out_shape=pltpu.VMEM((count,) + queries.shape[1:], BF16),
        in_specs=[pl.BlockSpec(memory_space=pltpu.HBM)],
        out_specs=pl.BlockSpec(memory_space=pltpu.VMEM),
        scratch_shapes=[pltpu.SemaphoreType.DMA],
        compiler_params=pltpu.CompilerParams(vmem_limit_bytes=2 << 20),
        cost_estimate=pl.CostEstimate(
            flops=0,
            bytes_accessed=2 * count * queries.shape[1] * queries.shape[2],
            transcendentals=0,
        ),
    )(pltpu.with_memory_space_constraint(queries, pltpu.HBM))


def score_kernel(piece, wide, parts, order_ref, *refs):
    grads, refs = refs[:wide], refs[wide:]
    here, (queries_ref, out_ref, held, sums, order, order_sem, sems) = refs[:parts], refs[parts:]
    rows, width = grads[0].shape
    total = queries_ref.shape[0]
    ready = total - held.shape[0]
    late = held.shape[0] // piece

    def copy(i):
        return pltpu.make_async_copy(
            queries_ref.at[pl.ds(ready + i * piece, piece)],
            held.at[pl.ds(i * piece, piece)],
            sems.at[i],
        )

    depth = 2
    for i in range(depth):
        copy(i).start()
    order_copy = pltpu.make_async_copy(order_ref, order, order_sem)
    order_copy.start()
    lanes = wide * GROUP
    weights = jnp.concatenate(
        [
            jnp.concatenate([grad[g : g + GROUP, :] for grad in grads], axis=0)
            for g in range(0, rows, GROUP)
        ],
        axis=1,
    )
    lane = lax.broadcasted_iota(jnp.int32, (GROUP, lanes), 1)
    diagonal = lax.broadcasted_iota(jnp.int32, (GROUP, lanes), 0) == lane % GROUP

    def products(source, first, count):
        block = jnp.concatenate(
            [
                source[pl.ds(first, count), g : g + GROUP, :].reshape(count * GROUP, width)
                for g in range(0, rows, GROUP)
            ],
            axis=1,
        )
        found = lax.dot_general(block, weights, NT, preferred_element_type=F32)
        kept = jnp.where(diagonal, found.reshape(count, GROUP, lanes), 0.0)
        return jnp.sum(kept, axis=1)

    done = 0
    for source in here:
        for first in range(0, source.shape[0], 80):
            sums[done : done + 80, :] = products(source, first, 80)
            done += 80

    def step(i, carry):
        copy(i).wait()

        @pl.when(i + depth < late)
        def _():
            copy(i + depth).start()

        for j in range(0, piece, 80):
            at = pl.multiple_of(i * piece + j, 16)
            sums[pl.ds(ready + at, 80), :] = products(held, at, 80)
        return carry

    lax.fori_loop(0, late, step, 0)

    order_copy.wait()
    row = lax.broadcasted_iota(jnp.int32, (2 * GROUP, lanes), 0)
    source = lax.broadcasted_iota(jnp.int32, (2 * GROUP, lanes), 1) // GROUP
    place = jnp.zeros((2 * GROUP, lanes), F32)
    for k in range(wide):
        goal = order[lax.axis_index("wide") ^ k]
        place += jnp.where((source == k) & (row == goal), 1.0, 0.0)
    place = place.astype(BF16)
    span = out_ref.shape[2]
    blocks = total // span
    for b in range(blocks):
        by_query = sums[b * span : (b + 1) * span, :]
        high = by_query.astype(BF16)
        low = (by_query - high.astype(F32)).astype(BF16)
        scores = lax.dot_general(place, high, NT, preferred_element_type=F32) + lax.dot_general(
            place, low, NT, preferred_element_type=F32
        )
        for m in range(wide):
            out_ref[m * blocks + b] = scores[m : m + 1]


def score_blocks(blocks, piece, order, grads, here, queries):
    wide = len(grads)
    total, rows, width = queries.shape
    late = total - sum(x.shape[0] for x in here)
    vmem = pl.BlockSpec(memory_space=pltpu.VMEM)
    return pl.pallas_call(
        functools.partial(score_kernel, piece, wide, len(here)),
        out_shape=jax.ShapeDtypeStruct((wide * blocks, 1, total // blocks), F32),
        in_specs=[pl.BlockSpec(memory_space=pl.ANY)]
        + [vmem] * (wide + len(here))
        + [pl.BlockSpec(memory_space=pltpu.HBM)],
        out_specs=vmem,
        scratch_shapes=[
            pltpu.VMEM((late, rows, width), BF16),
            pltpu.VMEM((total, wide * GROUP), F32),
            pltpu.SMEM(order.shape, jnp.int32),
            pltpu.SemaphoreType.DMA,
            pltpu.SemaphoreType.DMA((late // piece,)),
        ],
        compiler_params=pltpu.CompilerParams(vmem_limit_bytes=36 << 20),
        cost_estimate=pl.CostEstimate(
            flops=2 * total * rows * width * 128,
            bytes_accessed=2 * total * rows * width,
            transcendentals=0,
        ),
    )(
        order,
        *grads,
        *(pltpu.with_memory_space_constraint(x, pltpu.VMEM) for x in here),
        pltpu.with_memory_space_constraint(queries, pltpu.HBM),
    )


def shared(activations, deltas, act_factor, delta_factor, queries, assignment, padding):
    wide, rep, sub = (lax.axis_size(a) for a in ("wide", "rep", "sub"))
    half = act_factor.shape[1]
    own_block = lax.dynamic_slice_in_dim(act_factor, lax.axis_index("rep") * half, half, axis=0)
    far_block = lax.ppermute(own_block, "rep", [(0, 1), (1, 0)])
    early = queries.shape[0] // 8
    mine, columns, first = row_product(
        padding, deltas[0], activations[0], delta_factor, act_factor, queries, early
    )
    second = fetch(queries, early, early)
    mine, columns, far_block = lax.optimization_barrier((mine, columns, far_block))
    other = lax.ppermute(mine, "sub", [(0, 1), (1, 0)])
    sent = grad_blocks(wide, mine, other, columns, far_block)
    grads = [sent[0]] + [
        lax.ppermute(sent[k], "wide", [(i, i ^ k) for i in range(wide)]) for k in range(1, wide)
    ]
    partial = score_blocks(rep * sub, early, assignment, grads, [first, second], queries)
    gathered = lax.all_to_all(
        partial, ("wide", "rep", "sub"), split_axis=0, concat_axis=0, tiled=True
    )
    return jnp.sum(gathered, axis=0)


def general(activations, deltas, act_factor, delta_factor, queries, assignment, padding):
    seq_dev, tok_dev, _ = activations.shape
    full_length = tok_dev * lax.axis_size("sub")
    token_start = lax.axis_index("sub") * tok_dev
    positions = token_start + lax.broadcasted_iota(jnp.int32, (seq_dev, tok_dev), 1)
    kept_mask = positions < (full_length - padding)[:, None]
    masked = jnp.where(kept_mask[:, :, None], deltas, jnp.zeros((), BF16))
    delta_proj = jnp.einsum(
        "stw,wi->sti", masked, delta_factor, preferred_element_type=F32
    ).astype(BF16)
    act_proj = jnp.einsum(
        "stw,wj->stj",
        activations,
        lax.all_gather(act_factor, "rep", axis=1, tiled=True),
        preferred_element_type=F32,
    ).astype(BF16)
    partial_value = jnp.einsum("sti,stj->sij", delta_proj, act_proj, preferred_element_type=F32)
    summed = lax.psum_scatter(partial_value, "sub", scatter_dimension=2, tiled=True).astype(BF16)
    regrouped = lax.all_to_all(summed, "wide", split_axis=1, concat_axis=0, tiled=True)
    seq_total = regrouped.shape[0]
    grad_rows = regrouped.reshape(seq_total, -1)
    query_rows = queries.reshape(queries.shape[0], -1)
    partial_scores = lax.dot_general(grad_rows, query_rows, NT, preferred_element_type=F32)
    inverse_order = (
        jnp.zeros((seq_total,), jnp.int32)
        .at[assignment]
        .set(jnp.arange(seq_total, dtype=jnp.int32))
    )
    ranked = jnp.take(partial_scores, inverse_order, axis=0)
    by_column = lax.psum_scatter(ranked, ("rep", "sub"), scatter_dimension=1, tiled=True)
    return lax.psum_scatter(by_column, "wide", scatter_dimension=0, tiled=True)


def shards(activations, deltas, act_factor, delta_factor, queries, assignment, padding):
    wide, rep, sub = (lax.axis_size(a) for a in ("wide", "rep", "sub"))
    fits = (
        rep == 2
        and sub == 2
        and wide in (2, 4, 8)
        and activations.shape[:1] == (1,)
        and queries.shape[1] % GROUP == 0
        and queries.shape[0] % (16 * rep * sub) == 0
        and act_factor.shape[1] % 128 == 0
    )
    body = shared if fits else general
    return body(activations, deltas, act_factor, delta_factor, queries, assignment, padding)


def solution(mesh):
    placed = (
        P(("parts", "wide"), "sub", None),
        P(("parts", "wide"), "sub", None),
        P(None, "rep"),
        P(None, "rep"),
        P(None, ("rep", "wide"), "sub"),
        P("parts"),
        P(("parts", "wide")),
    )
    return jax.shard_map(
        shards,
        mesh=mesh,
        in_specs=placed,
        out_specs=P(("parts", "wide"), ("rep", "sub")),
        check_vma=False,
    )
```

```python
import functools

import jax
import jax.numpy as jnp
from jax import lax
from jax.experimental import pallas as pl
from jax.experimental.pallas import tpu as pltpu
from jax.sharding import PartitionSpec as P

GROUP = 16
F32 = jnp.float32
BF16 = jnp.bfloat16
NT = (((1,), (1,)), ((), ()))
TN = (((0,), (0,)), ((), ()))


def row_product_kernel(
    pad_ref, deltas_ref, acts_ref, row_factor_ref, col_factor_ref, queries_ref,
    out_ref, col_out_ref, early_ref,
    pad_in, deltas_in, acts_in, factor_in, sems,
):
    steps, tokens, _ = deltas_in.shape
    first = lax.axis_index("sub") * steps * tokens

    def copy(source, held, which, i):
        return pltpu.make_async_copy(
            source.at[pl.ds(i * tokens, tokens), :], held.at[i], sems.at[which, i]
        )

    row_copy = pltpu.make_async_copy(row_factor_ref, factor_in, sems.at[2, 0])
    col_copy = pltpu.make_async_copy(col_factor_ref, col_out_ref, sems.at[2, 1])
    pad_copy = pltpu.make_async_copy(pad_ref, pad_in, sems.at[2, 2])
    pad_copy.start()
    row_copy.start()
    for i in range(steps):
        copy(deltas_ref, deltas_in, 0, i).start()
        copy(acts_ref, acts_in, 1, i).start()
    col_copy.start()
    early_copy = pltpu.make_async_copy(
        queries_ref.at[pl.ds(0, early_ref.shape[0])], early_ref, sems.at[2, 3]
    )
    early_copy.start()
    out_ref[...] = jnp.zeros(out_ref.shape, F32)
    pad_copy.wait()
    row_copy.wait()
    limit = lax.axis_size("sub") * steps * tokens - pad_in[0]

    def step(i, carry):
        copy(deltas_ref, deltas_in, 0, i).wait()
        copy(acts_ref, acts_in, 1, i).wait()
        position = first + i * tokens + lax.broadcasted_iota(jnp.int32, (tokens, 1), 0)
        masked = jnp.where(position < limit, deltas_in[i], jnp.zeros((), BF16))
        proj = jnp.dot(masked, factor_in[...], preferred_element_type=F32).astype(BF16)
        out_ref[...] += lax.dot_general(proj, acts_in[i], TN, preferred_element_type=F32)
        return carry

    lax.fori_loop(0, steps, step, 0)
    col_copy.wait()
    early_copy.wait()


def row_product(padding, deltas, acts, row_factor, col_factor, queries, early):
    tokens, width = deltas.shape
    rows = row_factor.shape[1]
    steps = max(1, tokens // 512)
    hbm = pl.BlockSpec(memory_space=pltpu.HBM)
    vmem = pl.BlockSpec(memory_space=pltpu.VMEM)
    operands = [padding] + [
        pltpu.with_memory_space_constraint(x, pltpu.HBM)
        for x in (deltas, acts, row_factor, col_factor, queries)
    ]
    return pl.pallas_call(
        row_product_kernel,
        out_shape=(
            jax.ShapeDtypeStruct((rows, width), F32),
            jax.ShapeDtypeStruct(col_factor.shape, BF16),
            pltpu.VMEM((early,) + queries.shape[1:], BF16),
        ),
        in_specs=[pl.BlockSpec(memory_space=pl.ANY)] + [hbm] * 5,
        out_specs=(vmem, vmem, vmem),
        scratch_shapes=[
            pltpu.SMEM(padding.shape, jnp.int32),
            pltpu.VMEM((steps, tokens // steps, width), BF16),
            pltpu.VMEM((steps, tokens // steps, width), BF16),
            pltpu.VMEM(row_factor.shape, BF16),
            pltpu.SemaphoreType.DMA((3, max(4, steps))),
        ],
        compiler_params=pltpu.CompilerParams(vmem_limit_bytes=12 << 20),
        cost_estimate=pl.CostEstimate(
            flops=4 * tokens * width * rows, bytes_accessed=4 * tokens * width, transcendentals=0
        ),
    )(*operands)


def grad_kernel(wide, mine_ref, other_ref, factor_ref, far_ref, *outs_and_scratch):
    *outs, held = outs_and_scratch
    rep, sub, place = (lax.axis_index(a) for a in ("rep", "sub", "wide"))
    half = factor_ref.shape[1]
    rows = mine_ref.shape[0] // wide
    summed = mine_ref[...] + other_ref[...]
    high = summed.astype(BF16)
    low = (summed - high.astype(F32)).astype(BF16)

    @pl.when(rep == sub)
    def _():
        whole = factor_ref[...]
        held[...] = jnp.dot(high, whole, preferred_element_type=F32) + jnp.dot(
            low, whole, preferred_element_type=F32
        )

    for index in range(2):

        @pl.when((rep != sub) & (rep == index))
        def _():
            here = slice(index * half, (index + 1) * half)
            there = slice((1 - index) * half, (2 - index) * half)
            near, far = factor_ref[there, :], far_ref[...]
            held[...] = (
                lax.dot_general(high[:, here], near, NT, preferred_element_type=F32)
                + lax.dot_general(low[:, here], near, NT, preferred_element_type=F32)
                + jnp.dot(high[:, there], far, preferred_element_type=F32)
                + jnp.dot(low[:, there], far, preferred_element_type=F32)
            )

    for k in range(wide):
        start = pl.multiple_of((place ^ k) * rows, rows)
        outs[k][...] = held[pl.ds(start, rows), :].astype(BF16)


def grad_blocks(wide, mine, other, factor, far):
    rows, width = mine.shape
    half = factor.shape[1]
    vmem = pl.BlockSpec(memory_space=pltpu.VMEM)
    return pl.pallas_call(
        functools.partial(grad_kernel, wide),
        out_shape=[jax.ShapeDtypeStruct((rows // wide, half), BF16)] * wide,
        in_specs=[vmem] * 4,
        out_specs=[vmem] * wide,
        scratch_shapes=[pltpu.VMEM((rows, half), F32)],
        compiler_params=pltpu.CompilerParams(vmem_limit_bytes=8 << 20),
        cost_estimate=pl.CostEstimate(
            flops=4 * rows * width * half, bytes_accessed=12 * rows * width, transcendentals=0
        ),
    )(mine, other, factor, far)


def fetch_kernel(first, queries_ref, out_ref, sem):
    copy = pltpu.make_async_copy(queries_ref.at[pl.ds(first, out_ref.shape[0])], out_ref, sem)
    copy.start()
    copy.wait()


def fetch(queries, first, count):
    return pl.pallas_call(
        functools.partial(fetch_kernel, first),
        out_shape=pltpu.VMEM((count,) + queries.shape[1:], BF16),
        in_specs=[pl.BlockSpec(memory_space=pltpu.HBM)],
        out_specs=pl.BlockSpec(memory_space=pltpu.VMEM),
        scratch_shapes=[pltpu.SemaphoreType.DMA],
        compiler_params=pltpu.CompilerParams(vmem_limit_bytes=2 << 20),
        cost_estimate=pl.CostEstimate(
            flops=0,
            bytes_accessed=2 * count * queries.shape[1] * queries.shape[2],
            transcendentals=0,
        ),
    )(pltpu.with_memory_space_constraint(queries, pltpu.HBM))


def exchange_kernel(wide, order_ref, *refs):
    grads, (out_ref, order, sem) = refs[:wide], refs[wide:]
    rows, width = grads[0].shape
    part, parts = lax.axis_index("parts"), lax.axis_size("parts")
    share = rows // parts
    copy = pltpu.make_async_copy(order_ref, order, sem)
    copy.start()
    first = pl.multiple_of((1 - part) * share, share)
    for k in range(wide):
        out_ref[k * share : (k + 1) * share, :] = grads[k][pl.ds(first, share), :]
    copy.wait()
    row = lax.broadcasted_iota(jnp.int32, (GROUP, width), 0)
    lane = lax.broadcasted_iota(jnp.int32, (GROUP, width), 1)
    tags = jnp.zeros((GROUP, width), F32)
    for k in range(wide):
        goal = part * wide + order[lax.axis_index("wide") ^ k]
        tags += jnp.where((row == k) & (lane == goal), 1.0, 0.0)
    out_ref[wide * share :, :] = tags.astype(BF16)


def exchange_block(parts, order, grads):
    wide = len(grads)
    rows, width = grads[0].shape
    vmem = pl.BlockSpec(memory_space=pltpu.VMEM)
    return pl.pallas_call(
        functools.partial(exchange_kernel, wide),
        out_shape=jax.ShapeDtypeStruct((wide * rows // parts + GROUP, width), BF16),
        in_specs=[pl.BlockSpec(memory_space=pl.ANY)] + [vmem] * wide,
        out_specs=vmem,
        scratch_shapes=[pltpu.SMEM(order.shape, jnp.int32), pltpu.SemaphoreType.DMA],
        compiler_params=pltpu.CompilerParams(vmem_limit_bytes=2 << 20),
        cost_estimate=pl.CostEstimate(
            flops=0, bytes_accessed=4 * wide * rows * width, transcendentals=0
        ),
    )(order, *grads)


def joined_rows(source, first, count, start, rows):
    width = source.shape[2]
    return jnp.concatenate(
        [
            source[pl.ds(first, count), pl.ds(start + g, GROUP), :].reshape(count * GROUP, width)
            for g in range(0, rows, GROUP)
        ],
        axis=1,
    )


def group_sums(lines, weights, count):
    lanes = weights.shape[0]
    lane = lax.broadcasted_iota(jnp.int32, (GROUP, lanes), 1)
    diagonal = lax.broadcasted_iota(jnp.int32, (GROUP, lanes), 0) == lane % GROUP
    found = lax.dot_general(lines, weights, NT, preferred_element_type=F32)
    return jnp.sum(jnp.where(diagonal, found.reshape(count, GROUP, lanes), 0.0), axis=1)


def add_up(place, sums):
    high = sums.astype(BF16)
    low = (sums - high.astype(F32)).astype(BF16)
    return lax.dot_general(place, high, NT, preferred_element_type=F32) + lax.dot_general(
        place, low, NT, preferred_element_type=F32
    )


def place_of(block_ref, lanes, first):
    tags = block_ref[block_ref.shape[0] - GROUP :, :]
    source = lax.broadcasted_iota(jnp.int32, (GROUP, lanes), 1) // GROUP - first
    owner = source == lax.broadcasted_iota(jnp.int32, (GROUP, lanes), 0)
    return lax.dot_general(
        tags, owner.astype(F32).astype(BF16), TN, preferred_element_type=F32
    )[:GROUP]


LOOPS = 2


def local_score_kernel(wide, sets, tags_ref, *refs):
    grads, refs = refs[:wide], refs[wide:]
    here, (queries_ref, out_ref, held_ref, sums, sems) = refs[:sets], refs[sets:]
    rows, width = grads[0].shape
    part, parts = lax.axis_index("parts"), lax.axis_size("parts")
    share = rows // parts
    done = sum(source.shape[0] for source in here)
    half = held_ref.shape[0] // 2
    own = pl.multiple_of(part * share, share)

    def copy(i):
        return pltpu.make_async_copy(
            queries_ref.at[pl.ds(done + i * half, half), pl.ds(own, share), :],
            held_ref.at[pl.ds(i * half, half)],
            sems.at[i],
        )

    for i in range(2):
        copy(i).start()
    weights = jnp.concatenate(
        [
            jnp.concatenate([grad[g : g + GROUP, :] for grad in grads], axis=0)
            for g in range(0, rows, GROUP)
        ],
        axis=1,
    )
    def step(i, carry):
        counts = [source.shape[0] // LOOPS for source in here]
        lines = [
            joined_rows(source, pl.multiple_of(i * count, 8), count, 0, rows)
            for source, count in zip(here, counts)
        ]
        found = group_sums(jnp.concatenate(lines, axis=0), weights, sum(counts))
        at, taken = 0, 0
        for count in counts:
            to = pl.multiple_of(at + i * count, 8)
            sums[pl.ds(to, count), :] = found[taken : taken + count]
            at, taken = at + count * LOOPS, taken + count
        return carry

    lax.fori_loop(0, LOOPS, step, 0)
    out_ref[...] = add_up(place_of(tags_ref, wide * GROUP, 0).astype(BF16), sums[...])

    def finish(i, carry):
        copy(i).wait()
        return carry

    lax.fori_loop(0, 2, finish, 0)


def local_scores(parts, tagged, grads, here, queries, count):
    wide = len(grads)
    rows, width = grads[0].shape
    done = sum(x.shape[0] for x in here)
    vmem = pl.BlockSpec(memory_space=pltpu.VMEM)
    return pl.pallas_call(
        functools.partial(local_score_kernel, wide, len(here)),
        out_shape=(
            jax.ShapeDtypeStruct((GROUP, done), F32),
            pltpu.VMEM((count, rows // parts, width), BF16),
        ),
        in_specs=[vmem] * (1 + wide + len(here))
        + [pl.BlockSpec(memory_space=pltpu.HBM)],
        out_specs=(vmem, vmem),
        scratch_shapes=[
            pltpu.VMEM((done, wide * GROUP), F32),
            pltpu.SemaphoreType.DMA((2,)),
        ],
        compiler_params=pltpu.CompilerParams(vmem_limit_bytes=10 << 20),
        cost_estimate=pl.CostEstimate(
            flops=2 * done * rows * width * 128,
            bytes_accessed=2 * (done + count) * rows * width,
            transcendentals=0,
        ),
    )(
        tagged,
        *grads,
        *(pltpu.with_memory_space_constraint(x, pltpu.VMEM) for x in here),
        pltpu.with_memory_space_constraint(queries, pltpu.HBM),
    )


def shared_score_kernel(wide, pieces, tags_ref, *refs):
    grads, refs = refs[:wide], refs[wide:]
    far_ref, local_ref, here_ref, queries_ref, out_ref, held, sums, sems = refs
    rows, width = grads[0].shape
    part, parts = lax.axis_index("parts"), lax.axis_size("parts")
    share = rows // parts
    local = local_ref.shape[1]
    ready = here_ref.shape[0]
    piece = held.shape[0] // pieces
    own = pl.multiple_of(part * share, share)

    def copy(i):
        return pltpu.make_async_copy(
            queries_ref.at[pl.ds(local + ready + i * piece, piece), pl.ds(own, share), :],
            held.at[pl.ds(i * piece, piece)],
            sems.at[i],
        )

    depth = min(2, pieces)
    for i in range(depth):
        copy(i).start()
    lanes = parts * wide * GROUP
    weights = jnp.concatenate(
        [
            jnp.concatenate(
                [grad[pl.ds(own + g, GROUP), :] for grad in grads]
                + [far_ref[k * share + g : k * share + g + GROUP, :] for k in range(wide)],
                axis=0,
            )
            for g in range(0, share, GROUP)
        ],
        axis=1,
    )

    def ready_step(i, carry):
        at = pl.multiple_of(i * piece, GROUP)
        lines = joined_rows(here_ref, at, piece, 0, share)
        sums[pl.ds(local + at, piece), :] = group_sums(lines, weights, piece)
        return carry

    lax.fori_loop(0, ready // piece, ready_step, 0)

    def late_step(i, carry):
        copy(i).wait()

        @pl.when(i + depth < pieces)
        def _():
            copy(i + depth).start()

        at = pl.multiple_of(i * piece, GROUP)
        lines = joined_rows(held, at, piece, 0, share)
        sums[pl.ds(local + ready + at, piece), :] = group_sums(lines, weights, piece)
        return carry

    lax.fori_loop(0, pieces, late_step, 0)

    place = (place_of(tags_ref, lanes, 0) + place_of(far_ref, lanes, wide)).astype(BF16)
    span = out_ref.shape[2]
    blocks = queries_ref.shape[0] // span
    for b in range(blocks):
        if (b + 1) * span <= local:
            for m in range(parts * wide):
                out_ref[m * blocks + b] = local_ref[m : m + 1, b * span : (b + 1) * span]
        else:
            scores = add_up(place, sums[b * span : (b + 1) * span, :])
            for m in range(parts * wide):
                out_ref[m * blocks + b] = scores[m : m + 1]


def shared_scores(parts, blocks, pieces, tagged, grads, far, local, here, queries):
    wide = len(grads)
    rows, width = grads[0].shape
    total = queries.shape[0]
    late = total - local.shape[1] - here.shape[0]
    vmem = pl.BlockSpec(memory_space=pltpu.VMEM)
    return pl.pallas_call(
        functools.partial(shared_score_kernel, wide, pieces),
        out_shape=jax.ShapeDtypeStruct((parts * wide * blocks, 1, total // blocks), F32),
        in_specs=[vmem] * (wide + 4)
        + [pl.BlockSpec(memory_space=pltpu.HBM)],
        out_specs=vmem,
        scratch_shapes=[
            pltpu.VMEM((late, rows // parts, width), BF16),
            pltpu.VMEM((total, parts * wide * GROUP), F32),
            pltpu.SemaphoreType.DMA((pieces,)),
        ],
        compiler_params=pltpu.CompilerParams(vmem_limit_bytes=20 << 20),
        cost_estimate=pl.CostEstimate(
            flops=2 * total * rows * width * 128,
            bytes_accessed=2 * late * rows * width,
            transcendentals=0,
        ),
    )(
        tagged,
        *grads,
        far,
        local,
        pltpu.with_memory_space_constraint(here, pltpu.VMEM),
        pltpu.with_memory_space_constraint(queries, pltpu.HBM),
    )


def shared(activations, deltas, act_factor, delta_factor, queries, assignment, padding):
    parts, wide, rep, sub = (lax.axis_size(a) for a in ("parts", "wide", "rep", "sub"))
    half = act_factor.shape[1]
    early = queries.shape[0] // 8
    later = 3 * early
    own_block = lax.dynamic_slice_in_dim(act_factor, lax.axis_index("rep") * half, half, axis=0)
    far_block = lax.ppermute(own_block, "rep", [(0, 1), (1, 0)])
    mine, columns, first = row_product(
        padding, deltas[0], activations[0], delta_factor, act_factor, queries, early
    )
    second = fetch(queries, early, early // 2)
    third = fetch(queries, 3 * early // 2, early // 2)
    mine, columns, far_block = lax.optimization_barrier((mine, columns, far_block))
    other = lax.ppermute(mine, "sub", [(0, 1), (1, 0)])
    other, second = lax.optimization_barrier((other, second))
    sent = grad_blocks(wide, mine, other, columns, far_block)
    grads = [sent[0]] + [
        lax.ppermute(sent[k], "wide", [(i, i ^ k) for i in range(wide)]) for k in range(1, wide)
    ]
    tagged = exchange_block(parts, assignment, grads)
    far = lax.ppermute(tagged, "parts", [(0, 1), (1, 0)])
    local, held = local_scores(
        parts, tagged, grads, [first, second, third], queries, later
    )
    partial = shared_scores(
        parts, rep * sub, 3, tagged, grads, far, local, held, queries
    )
    gathered = lax.all_to_all(
        partial, ("parts", "wide", "rep", "sub"), split_axis=0, concat_axis=0, tiled=True
    )
    return jnp.sum(gathered, axis=0)


def general(activations, deltas, act_factor, delta_factor, queries, assignment, padding):
    seq_dev, tok_dev, _ = activations.shape
    full_length = tok_dev * lax.axis_size("sub")
    token_start = lax.axis_index("sub") * tok_dev
    positions = token_start + lax.broadcasted_iota(jnp.int32, (seq_dev, tok_dev), 1)
    kept_mask = positions < (full_length - padding)[:, None]
    masked = jnp.where(kept_mask[:, :, None], deltas, jnp.zeros((), BF16))
    delta_proj = jnp.einsum(
        "stw,wi->sti", masked, delta_factor, preferred_element_type=F32
    ).astype(BF16)
    act_proj = jnp.einsum(
        "stw,wj->stj",
        activations,
        lax.all_gather(act_factor, "rep", axis=1, tiled=True),
        preferred_element_type=F32,
    ).astype(BF16)
    partial_value = jnp.einsum("sti,stj->sij", delta_proj, act_proj, preferred_element_type=F32)
    summed = lax.psum_scatter(partial_value, "sub", scatter_dimension=2, tiled=True).astype(BF16)
    regrouped = lax.all_to_all(summed, "wide", split_axis=1, concat_axis=0, tiled=True)
    seq_total = regrouped.shape[0]
    grad_rows = regrouped.reshape(seq_total, -1)
    query_rows = queries.reshape(queries.shape[0], -1)
    partial_scores = lax.dot_general(grad_rows, query_rows, NT, preferred_element_type=F32)
    inverse_order = (
        jnp.zeros((seq_total,), jnp.int32)
        .at[assignment]
        .set(jnp.arange(seq_total, dtype=jnp.int32))
    )
    ranked = jnp.take(partial_scores, inverse_order, axis=0)
    by_column = lax.psum_scatter(ranked, ("rep", "sub"), scatter_dimension=1, tiled=True)
    return lax.psum_scatter(by_column, "wide", scatter_dimension=0, tiled=True)


def shards(activations, deltas, act_factor, delta_factor, queries, assignment, padding):
    parts, wide, rep, sub = (lax.axis_size(a) for a in ("parts", "wide", "rep", "sub"))
    fits = (
        parts == 2
        and rep == 2
        and sub == 2
        and wide in (2, 4)
        and activations.shape[0] == 1
        and queries.shape[1] % (parts * GROUP) == 0
        and queries.shape[0] % (16 * GROUP) == 0
        and act_factor.shape[1] % 128 == 0
    )
    body = shared if fits else general
    return body(activations, deltas, act_factor, delta_factor, queries, assignment, padding)


def solution(mesh):
    placed = (
        P(("parts", "wide"), "sub", None),
        P(("parts", "wide"), "sub", None),
        P(None, "rep"),
        P(None, "rep"),
        P(None, ("rep", "wide"), "sub"),
        P("parts"),
        P(("parts", "wide")),
    )
    return jax.shard_map(
        shards,
        mesh=mesh,
        in_specs=placed,
        out_specs=P(("parts", "wide"), ("rep", "sub")),
        check_vma=False,
    )
```

```python
import functools

import jax
import jax.numpy as jnp
from jax import lax
from jax.experimental import pallas as pl
from jax.experimental.pallas import tpu as pltpu
from jax.sharding import PartitionSpec as P

GROUP = 16
F32 = jnp.float32
BF16 = jnp.bfloat16
NT = (((1,), (1,)), ((), ()))
TN = (((0,), (0,)), ((), ()))


def row_product_kernel(
    pad_ref, deltas_ref, acts_ref, row_factor_ref, col_factor_ref, queries_ref,
    out_ref, col_out_ref, early_ref,
    pad_in, deltas_in, acts_in, factor_in, sems,
):
    steps, tokens, _ = deltas_in.shape
    first = lax.axis_index("sub") * steps * tokens

    def copy(source, held, which, i):
        return pltpu.make_async_copy(
            source.at[pl.ds(i * tokens, tokens), :], held.at[i], sems.at[which, i]
        )

    row_copy = pltpu.make_async_copy(row_factor_ref, factor_in, sems.at[2, 0])
    col_copy = pltpu.make_async_copy(col_factor_ref, col_out_ref, sems.at[2, 1])
    pad_copy = pltpu.make_async_copy(pad_ref, pad_in, sems.at[2, 2])
    pad_copy.start()
    row_copy.start()
    for i in range(steps):
        copy(deltas_ref, deltas_in, 0, i).start()
        copy(acts_ref, acts_in, 1, i).start()
    col_copy.start()
    early_copy = pltpu.make_async_copy(
        queries_ref.at[pl.ds(0, early_ref.shape[0])], early_ref, sems.at[2, 3]
    )
    early_copy.start()
    out_ref[...] = jnp.zeros(out_ref.shape, F32)
    pad_copy.wait()
    row_copy.wait()
    limit = lax.axis_size("sub") * steps * tokens - pad_in[0]

    def step(i, carry):
        copy(deltas_ref, deltas_in, 0, i).wait()
        copy(acts_ref, acts_in, 1, i).wait()
        position = first + i * tokens + lax.broadcasted_iota(jnp.int32, (tokens, 1), 0)
        masked = jnp.where(position < limit, deltas_in[i], jnp.zeros((), BF16))
        proj = jnp.dot(masked, factor_in[...], preferred_element_type=F32).astype(BF16)
        out_ref[...] += lax.dot_general(proj, acts_in[i], TN, preferred_element_type=F32)
        return carry

    lax.fori_loop(0, steps, step, 0)
    col_copy.wait()
    early_copy.wait()


def row_product(padding, deltas, acts, row_factor, col_factor, queries, early):
    tokens, width = deltas.shape
    rows = row_factor.shape[1]
    steps = max(1, tokens // 512)
    hbm = pl.BlockSpec(memory_space=pltpu.HBM)
    vmem = pl.BlockSpec(memory_space=pltpu.VMEM)
    operands = [padding] + [
        pltpu.with_memory_space_constraint(x, pltpu.HBM)
        for x in (deltas, acts, row_factor, col_factor, queries)
    ]
    return pl.pallas_call(
        row_product_kernel,
        out_shape=(
            jax.ShapeDtypeStruct((rows, width), F32),
            jax.ShapeDtypeStruct(col_factor.shape, BF16),
            pltpu.VMEM((early,) + queries.shape[1:], BF16),
        ),
        in_specs=[pl.BlockSpec(memory_space=pl.ANY)] + [hbm] * 5,
        out_specs=(vmem, vmem, vmem),
        scratch_shapes=[
            pltpu.SMEM(padding.shape, jnp.int32),
            pltpu.VMEM((steps, tokens // steps, width), BF16),
            pltpu.VMEM((steps, tokens // steps, width), BF16),
            pltpu.VMEM(row_factor.shape, BF16),
            pltpu.SemaphoreType.DMA((3, max(4, steps))),
        ],
        compiler_params=pltpu.CompilerParams(vmem_limit_bytes=12 << 20),
        cost_estimate=pl.CostEstimate(
            flops=4 * tokens * width * rows, bytes_accessed=4 * tokens * width, transcendentals=0
        ),
    )(*operands)


def grad_kernel(wide, mine_ref, other_ref, factor_ref, far_ref, *outs_and_scratch):
    *outs, held = outs_and_scratch
    rep, sub, place = (lax.axis_index(a) for a in ("rep", "sub", "wide"))
    half = factor_ref.shape[1]
    rows = mine_ref.shape[0] // wide
    summed = mine_ref[...] + other_ref[...]
    high = summed.astype(BF16)
    low = (summed - high.astype(F32)).astype(BF16)

    @pl.when(rep == sub)
    def _():
        whole = factor_ref[...]
        held[...] = jnp.dot(high, whole, preferred_element_type=F32) + jnp.dot(
            low, whole, preferred_element_type=F32
        )

    for index in range(2):

        @pl.when((rep != sub) & (rep == index))
        def _():
            here = slice(index * half, (index + 1) * half)
            there = slice((1 - index) * half, (2 - index) * half)
            near, far = factor_ref[there, :], far_ref[...]
            held[...] = (
                lax.dot_general(high[:, here], near, NT, preferred_element_type=F32)
                + lax.dot_general(low[:, here], near, NT, preferred_element_type=F32)
                + jnp.dot(high[:, there], far, preferred_element_type=F32)
                + jnp.dot(low[:, there], far, preferred_element_type=F32)
            )

    for k in range(wide):
        start = pl.multiple_of((place ^ k) * rows, rows)
        outs[k][...] = held[pl.ds(start, rows), :].astype(BF16)


def grad_blocks(wide, mine, other, factor, far):
    rows, width = mine.shape
    half = factor.shape[1]
    vmem = pl.BlockSpec(memory_space=pltpu.VMEM)
    return pl.pallas_call(
        functools.partial(grad_kernel, wide),
        out_shape=[jax.ShapeDtypeStruct((rows // wide, half), BF16)] * wide,
        in_specs=[vmem] * 4,
        out_specs=[vmem] * wide,
        scratch_shapes=[pltpu.VMEM((rows, half), F32)],
        compiler_params=pltpu.CompilerParams(vmem_limit_bytes=8 << 20),
        cost_estimate=pl.CostEstimate(
            flops=4 * rows * width * half, bytes_accessed=12 * rows * width, transcendentals=0
        ),
    )(mine, other, factor, far)


def fetch_kernel(first, queries_ref, out_ref, sem):
    copy = pltpu.make_async_copy(queries_ref.at[pl.ds(first, out_ref.shape[0])], out_ref, sem)
    copy.start()
    copy.wait()


def fetch(queries, first, count):
    return pl.pallas_call(
        functools.partial(fetch_kernel, first),
        out_shape=pltpu.VMEM((count,) + queries.shape[1:], BF16),
        in_specs=[pl.BlockSpec(memory_space=pltpu.HBM)],
        out_specs=pl.BlockSpec(memory_space=pltpu.VMEM),
        scratch_shapes=[pltpu.SemaphoreType.DMA],
        compiler_params=pltpu.CompilerParams(vmem_limit_bytes=2 << 20),
        cost_estimate=pl.CostEstimate(
            flops=0,
            bytes_accessed=2 * count * queries.shape[1] * queries.shape[2],
            transcendentals=0,
        ),
    )(pltpu.with_memory_space_constraint(queries, pltpu.HBM))


def exchange_kernel(wide, order_ref, *refs):
    grads, (out_ref, order, sem) = refs[:wide], refs[wide:]
    rows, width = grads[0].shape
    part, parts = lax.axis_index("parts"), lax.axis_size("parts")
    share = rows // parts
    copy = pltpu.make_async_copy(order_ref, order, sem)
    copy.start()
    first = pl.multiple_of((1 - part) * share, share)
    for k in range(wide):
        out_ref[k * share : (k + 1) * share, :] = grads[k][pl.ds(first, share), :]
    copy.wait()
    row = lax.broadcasted_iota(jnp.int32, (GROUP, width), 0)
    lane = lax.broadcasted_iota(jnp.int32, (GROUP, width), 1)
    tags = jnp.zeros((GROUP, width), F32)
    for k in range(wide):
        goal = part * wide + order[lax.axis_index("wide") ^ k]
        tags += jnp.where((row == k) & (lane == goal), 1.0, 0.0)
    out_ref[wide * share :, :] = tags.astype(BF16)


def exchange_block(parts, order, grads):
    wide = len(grads)
    rows, width = grads[0].shape
    vmem = pl.BlockSpec(memory_space=pltpu.VMEM)
    return pl.pallas_call(
        functools.partial(exchange_kernel, wide),
        out_shape=jax.ShapeDtypeStruct((wide * rows // parts + GROUP, width), BF16),
        in_specs=[pl.BlockSpec(memory_space=pl.ANY)] + [vmem] * wide,
        out_specs=vmem,
        scratch_shapes=[pltpu.SMEM(order.shape, jnp.int32), pltpu.SemaphoreType.DMA],
        compiler_params=pltpu.CompilerParams(vmem_limit_bytes=2 << 20),
        cost_estimate=pl.CostEstimate(
            flops=0, bytes_accessed=4 * wide * rows * width, transcendentals=0
        ),
    )(order, *grads)


def joined_rows(source, first, count, start, rows):
    width = source.shape[2]
    return jnp.concatenate(
        [
            source[pl.ds(first, count), pl.ds(start + g, GROUP), :].reshape(count * GROUP, width)
            for g in range(0, rows, GROUP)
        ],
        axis=1,
    )


def group_sums(lines, weights, count):
    lanes = weights.shape[0]
    lane = lax.broadcasted_iota(jnp.int32, (GROUP, lanes), 1)
    diagonal = lax.broadcasted_iota(jnp.int32, (GROUP, lanes), 0) == lane % GROUP
    found = lax.dot_general(lines, weights, NT, preferred_element_type=F32)
    return jnp.sum(jnp.where(diagonal, found.reshape(count, GROUP, lanes), 0.0), axis=1)


def add_up(place, sums):
    high = sums.astype(BF16)
    low = (sums - high.astype(F32)).astype(BF16)
    return lax.dot_general(place, high, NT, preferred_element_type=F32) + lax.dot_general(
        place, low, NT, preferred_element_type=F32
    )


def place_of(block_ref, lanes, first):
    tags = block_ref[block_ref.shape[0] - GROUP :, :]
    source = lax.broadcasted_iota(jnp.int32, (GROUP, lanes), 1) // GROUP - first
    owner = source == lax.broadcasted_iota(jnp.int32, (GROUP, lanes), 0)
    return lax.dot_general(
        tags, owner.astype(F32).astype(BF16), TN, preferred_element_type=F32
    )[:GROUP]


LOOPS = 2


def local_score_kernel(wide, sets, tags_ref, *refs):
    grads, refs = refs[:wide], refs[wide:]
    here, (queries_ref, out_ref, held_ref, sums, sems) = refs[:sets], refs[sets:]
    rows, width = grads[0].shape
    part, parts = lax.axis_index("parts"), lax.axis_size("parts")
    share = rows // parts
    done = sum(source.shape[0] for source in here)
    half = held_ref.shape[0] // 2
    own = pl.multiple_of(part * share, share)

    def copy(i):
        return pltpu.make_async_copy(
            queries_ref.at[pl.ds(done + i * half, half), pl.ds(own, share), :],
            held_ref.at[pl.ds(i * half, half)],
            sems.at[i],
        )

    for i in range(2):
        copy(i).start()
    weights = jnp.concatenate(
        [
            jnp.concatenate([grad[g : g + GROUP, :] for grad in grads], axis=0)
            for g in range(0, rows, GROUP)
        ],
        axis=1,
    )
    def step(i, carry):
        counts = [source.shape[0] // LOOPS for source in here]
        lines = [
            joined_rows(source, pl.multiple_of(i * count, 8), count, 0, rows)
            for source, count in zip(here, counts)
        ]
        found = group_sums(jnp.concatenate(lines, axis=0), weights, sum(counts))
        at, taken = 0, 0
        for count in counts:
            to = pl.multiple_of(at + i * count, 8)
            sums[pl.ds(to, count), :] = found[taken : taken + count]
            at, taken = at + count * LOOPS, taken + count
        return carry

    lax.fori_loop(0, LOOPS, step, 0)
    out_ref[...] = add_up(place_of(tags_ref, wide * GROUP, 0).astype(BF16), sums[...])

    def finish(i, carry):
        copy(i).wait()
        return carry

    lax.fori_loop(0, 2, finish, 0)


def local_scores(parts, tagged, grads, here, queries, count):
    wide = len(grads)
    rows, width = grads[0].shape
    done = sum(x.shape[0] for x in here)
    vmem = pl.BlockSpec(memory_space=pltpu.VMEM)
    return pl.pallas_call(
        functools.partial(local_score_kernel, wide, len(here)),
        out_shape=(
            jax.ShapeDtypeStruct((GROUP, done), F32),
            pltpu.VMEM((count, rows // parts, width), BF16),
        ),
        in_specs=[vmem] * (1 + wide + len(here))
        + [pl.BlockSpec(memory_space=pltpu.HBM)],
        out_specs=(vmem, vmem),
        scratch_shapes=[
            pltpu.VMEM((done, wide * GROUP), F32),
            pltpu.SemaphoreType.DMA((2,)),
        ],
        compiler_params=pltpu.CompilerParams(vmem_limit_bytes=10 << 20),
        cost_estimate=pl.CostEstimate(
            flops=2 * done * rows * width * 128,
            bytes_accessed=2 * (done + count) * rows * width,
            transcendentals=0,
        ),
    )(
        tagged,
        *grads,
        *(pltpu.with_memory_space_constraint(x, pltpu.VMEM) for x in here),
        pltpu.with_memory_space_constraint(queries, pltpu.HBM),
    )


def shared_score_kernel(wide, pieces, tags_ref, *refs):
    grads, refs = refs[:wide], refs[wide:]
    far_ref, local_ref, here_ref, queries_ref, out_ref, held, sums, sems = refs
    rows, width = grads[0].shape
    part, parts = lax.axis_index("parts"), lax.axis_size("parts")
    share = rows // parts
    local = local_ref.shape[1]
    ready = here_ref.shape[0]
    piece = held.shape[0] // pieces
    own = pl.multiple_of(part * share, share)

    def copy(i):
        return pltpu.make_async_copy(
            queries_ref.at[pl.ds(local + ready + i * piece, piece), pl.ds(own, share), :],
            held.at[pl.ds(i * piece, piece)],
            sems.at[i],
        )

    depth = min(2, pieces)
    for i in range(depth):
        copy(i).start()
    lanes = parts * wide * GROUP
    weights = jnp.concatenate(
        [
            jnp.concatenate(
                [grad[pl.ds(own + g, GROUP), :] for grad in grads]
                + [far_ref[k * share + g : k * share + g + GROUP, :] for k in range(wide)],
                axis=0,
            )
            for g in range(0, share, GROUP)
        ],
        axis=1,
    )

    def ready_step(i, carry):
        at = pl.multiple_of(i * piece, GROUP)
        lines = joined_rows(here_ref, at, piece, 0, share)
        sums[pl.ds(local + at, piece), :] = group_sums(lines, weights, piece)
        return carry

    lax.fori_loop(0, ready // piece, ready_step, 0)

    def late_step(i, carry):
        copy(i).wait()

        @pl.when(i + depth < pieces)
        def _():
            copy(i + depth).start()

        at = pl.multiple_of(i * piece, GROUP)
        lines = joined_rows(held, at, piece, 0, share)
        sums[pl.ds(local + ready + at, piece), :] = group_sums(lines, weights, piece)
        return carry

    lax.fori_loop(0, pieces, late_step, 0)

    place = (place_of(tags_ref, lanes, 0) + place_of(far_ref, lanes, wide)).astype(BF16)
    span = out_ref.shape[2]
    blocks = queries_ref.shape[0] // span
    for b in range(blocks):
        if (b + 1) * span <= local:
            for m in range(parts * wide):
                out_ref[m * blocks + b] = local_ref[m : m + 1, b * span : (b + 1) * span]
        else:
            scores = add_up(place, sums[b * span : (b + 1) * span, :])
            for m in range(parts * wide):
                out_ref[m * blocks + b] = scores[m : m + 1]


def shared_scores(parts, blocks, pieces, tagged, grads, far, local, here, queries):
    wide = len(grads)
    rows, width = grads[0].shape
    total = queries.shape[0]
    late = total - local.shape[1] - here.shape[0]
    vmem = pl.BlockSpec(memory_space=pltpu.VMEM)
    return pl.pallas_call(
        functools.partial(shared_score_kernel, wide, pieces),
        out_shape=jax.ShapeDtypeStruct((parts * wide * blocks, 1, total // blocks), F32),
        in_specs=[vmem] * (wide + 4)
        + [pl.BlockSpec(memory_space=pltpu.HBM)],
        out_specs=vmem,
        scratch_shapes=[
            pltpu.VMEM((late, rows // parts, width), BF16),
            pltpu.VMEM((total, parts * wide * GROUP), F32),
            pltpu.SemaphoreType.DMA((pieces,)),
        ],
        compiler_params=pltpu.CompilerParams(vmem_limit_bytes=20 << 20),
        cost_estimate=pl.CostEstimate(
            flops=2 * total * rows * width * 128,
            bytes_accessed=2 * late * rows * width,
            transcendentals=0,
        ),
    )(
        tagged,
        *grads,
        far,
        local,
        pltpu.with_memory_space_constraint(here, pltpu.VMEM),
        pltpu.with_memory_space_constraint(queries, pltpu.HBM),
    )


def shared(activations, deltas, act_factor, delta_factor, queries, assignment, padding):
    parts, wide, rep, sub = (lax.axis_size(a) for a in ("parts", "wide", "rep", "sub"))
    half = act_factor.shape[1]
    early = queries.shape[0] // 8
    later = 3 * early
    own_block = lax.dynamic_slice_in_dim(act_factor, lax.axis_index("rep") * half, half, axis=0)
    far_block = lax.ppermute(own_block, "rep", [(0, 1), (1, 0)])
    mine, columns, first = row_product(
        padding, deltas[0], activations[0], delta_factor, act_factor, queries, early
    )
    second = fetch(queries, early, early // 2)
    third = fetch(queries, 3 * early // 2, early // 2)
    mine, columns, far_block = lax.optimization_barrier((mine, columns, far_block))
    other = lax.ppermute(mine, "sub", [(0, 1), (1, 0)])
    other, second = lax.optimization_barrier((other, second))
    sent = grad_blocks(wide, mine, other, columns, far_block)
    grads = [sent[0]] + [
        lax.ppermute(sent[k], "wide", [(i, i ^ k) for i in range(wide)]) for k in range(1, wide)
    ]
    tagged = exchange_block(parts, assignment, grads)
    far = lax.ppermute(tagged, "parts", [(0, 1), (1, 0)])
    local, held = local_scores(
        parts, tagged, grads, [first, second, third], queries, later
    )
    partial = shared_scores(
        parts, rep * sub, 2, tagged, grads, far, local, held, queries
    )
    gathered = lax.all_to_all(
        partial, ("parts", "wide", "rep", "sub"), split_axis=0, concat_axis=0, tiled=True
    )
    return jnp.sum(gathered, axis=0)


def general(activations, deltas, act_factor, delta_factor, queries, assignment, padding):
    seq_dev, tok_dev, _ = activations.shape
    full_length = tok_dev * lax.axis_size("sub")
    token_start = lax.axis_index("sub") * tok_dev
    positions = token_start + lax.broadcasted_iota(jnp.int32, (seq_dev, tok_dev), 1)
    kept_mask = positions < (full_length - padding)[:, None]
    masked = jnp.where(kept_mask[:, :, None], deltas, jnp.zeros((), BF16))
    delta_proj = jnp.einsum(
        "stw,wi->sti", masked, delta_factor, preferred_element_type=F32
    ).astype(BF16)
    act_proj = jnp.einsum(
        "stw,wj->stj",
        activations,
        lax.all_gather(act_factor, "rep", axis=1, tiled=True),
        preferred_element_type=F32,
    ).astype(BF16)
    partial_value = jnp.einsum("sti,stj->sij", delta_proj, act_proj, preferred_element_type=F32)
    summed = lax.psum_scatter(partial_value, "sub", scatter_dimension=2, tiled=True).astype(BF16)
    regrouped = lax.all_to_all(summed, "wide", split_axis=1, concat_axis=0, tiled=True)
    seq_total = regrouped.shape[0]
    grad_rows = regrouped.reshape(seq_total, -1)
    query_rows = queries.reshape(queries.shape[0], -1)
    partial_scores = lax.dot_general(grad_rows, query_rows, NT, preferred_element_type=F32)
    inverse_order = (
        jnp.zeros((seq_total,), jnp.int32)
        .at[assignment]
        .set(jnp.arange(seq_total, dtype=jnp.int32))
    )
    ranked = jnp.take(partial_scores, inverse_order, axis=0)
    by_column = lax.psum_scatter(ranked, ("rep", "sub"), scatter_dimension=1, tiled=True)
    return lax.psum_scatter(by_column, "wide", scatter_dimension=0, tiled=True)


def shards(activations, deltas, act_factor, delta_factor, queries, assignment, padding):
    parts, wide, rep, sub = (lax.axis_size(a) for a in ("parts", "wide", "rep", "sub"))
    fits = (
        parts == 2
        and rep == 2
        and sub == 2
        and wide in (2, 4)
        and activations.shape[0] == 1
        and queries.shape[1] % (parts * GROUP) == 0
        and queries.shape[0] % (16 * GROUP) == 0
        and act_factor.shape[1] % 128 == 0
    )
    body = shared if fits else general
    return body(activations, deltas, act_factor, delta_factor, queries, assignment, padding)


def solution(mesh):
    placed = (
        P(("parts", "wide"), "sub", None),
        P(("parts", "wide"), "sub", None),
        P(None, "rep"),
        P(None, "rep"),
        P(None, ("rep", "wide"), "sub"),
        P("parts"),
        P(("parts", "wide")),
    )
    return jax.shard_map(
        shards,
        mesh=mesh,
        in_specs=placed,
        out_specs=P(("parts", "wide"), ("rep", "sub")),
        check_vma=False,
    )
```

```python
import functools

import jax
import jax.numpy as jnp
from jax import lax
from jax.experimental import pallas as pl
from jax.experimental.pallas import tpu as pltpu
from jax.sharding import PartitionSpec as P

GROUP = 16
F32 = jnp.float32
BF16 = jnp.bfloat16
NT = (((1,), (1,)), ((), ()))
TN = (((0,), (0,)), ((), ()))


def row_product_kernel(
    pad_ref, deltas_ref, acts_ref, row_factor_ref, col_factor_ref, queries_ref,
    out_ref, col_out_ref, early_ref,
    pad_in, deltas_in, acts_in, factor_in, sems,
):
    steps, tokens, _ = deltas_in.shape
    first = lax.axis_index("sub") * steps * tokens

    def copy(source, held, which, i):
        return pltpu.make_async_copy(
            source.at[pl.ds(i * tokens, tokens), :], held.at[i], sems.at[which, i]
        )

    row_copy = pltpu.make_async_copy(row_factor_ref, factor_in, sems.at[2, 0])
    col_copy = pltpu.make_async_copy(col_factor_ref, col_out_ref, sems.at[2, 1])
    pad_copy = pltpu.make_async_copy(pad_ref, pad_in, sems.at[2, 2])
    pad_copy.start()
    row_copy.start()
    for i in range(steps):
        copy(deltas_ref, deltas_in, 0, i).start()
        copy(acts_ref, acts_in, 1, i).start()
    col_copy.start()
    early_copy = pltpu.make_async_copy(
        queries_ref.at[pl.ds(0, early_ref.shape[0])], early_ref, sems.at[2, 3]
    )
    early_copy.start()
    out_ref[...] = jnp.zeros(out_ref.shape, F32)
    pad_copy.wait()
    row_copy.wait()
    limit = lax.axis_size("sub") * steps * tokens - pad_in[0]

    def step(i, carry):
        copy(deltas_ref, deltas_in, 0, i).wait()
        copy(acts_ref, acts_in, 1, i).wait()
        position = first + i * tokens + lax.broadcasted_iota(jnp.int32, (tokens, 1), 0)
        masked = jnp.where(position < limit, deltas_in[i], jnp.zeros((), BF16))
        proj = jnp.dot(masked, factor_in[...], preferred_element_type=F32).astype(BF16)
        out_ref[...] += lax.dot_general(proj, acts_in[i], TN, preferred_element_type=F32)
        return carry

    lax.fori_loop(0, steps, step, 0)
    col_copy.wait()
    early_copy.wait()


def row_product(padding, deltas, acts, row_factor, col_factor, queries, early):
    tokens, width = deltas.shape
    rows = row_factor.shape[1]
    steps = max(1, tokens // 512)
    hbm = pl.BlockSpec(memory_space=pltpu.HBM)
    vmem = pl.BlockSpec(memory_space=pltpu.VMEM)
    operands = [padding] + [
        pltpu.with_memory_space_constraint(x, pltpu.HBM)
        for x in (deltas, acts, row_factor, col_factor, queries)
    ]
    return pl.pallas_call(
        row_product_kernel,
        out_shape=(
            jax.ShapeDtypeStruct((rows, width), F32),
            jax.ShapeDtypeStruct(col_factor.shape, BF16),
            pltpu.VMEM((early,) + queries.shape[1:], BF16),
        ),
        in_specs=[pl.BlockSpec(memory_space=pl.ANY)] + [hbm] * 5,
        out_specs=(vmem, vmem, vmem),
        scratch_shapes=[
            pltpu.SMEM(padding.shape, jnp.int32),
            pltpu.VMEM((steps, tokens // steps, width), BF16),
            pltpu.VMEM((steps, tokens // steps, width), BF16),
            pltpu.VMEM(row_factor.shape, BF16),
            pltpu.SemaphoreType.DMA((3, max(4, steps))),
        ],
        compiler_params=pltpu.CompilerParams(vmem_limit_bytes=12 << 20),
        cost_estimate=pl.CostEstimate(
            flops=4 * tokens * width * rows, bytes_accessed=4 * tokens * width, transcendentals=0
        ),
    )(*operands)


def grad_kernel(wide, mine_ref, other_ref, factor_ref, far_ref, *outs_and_scratch):
    *outs, held = outs_and_scratch
    rep, sub, place = (lax.axis_index(a) for a in ("rep", "sub", "wide"))
    half = factor_ref.shape[1]
    rows = mine_ref.shape[0] // wide
    summed = mine_ref[...] + other_ref[...]
    high = summed.astype(BF16)
    low = (summed - high.astype(F32)).astype(BF16)

    @pl.when(rep == sub)
    def _():
        whole = factor_ref[...]
        held[...] = jnp.dot(high, whole, preferred_element_type=F32) + jnp.dot(
            low, whole, preferred_element_type=F32
        )

    for index in range(2):

        @pl.when((rep != sub) & (rep == index))
        def _():
            here = slice(index * half, (index + 1) * half)
            there = slice((1 - index) * half, (2 - index) * half)
            near, far = factor_ref[there, :], far_ref[...]
            held[...] = (
                lax.dot_general(high[:, here], near, NT, preferred_element_type=F32)
                + lax.dot_general(low[:, here], near, NT, preferred_element_type=F32)
                + jnp.dot(high[:, there], far, preferred_element_type=F32)
                + jnp.dot(low[:, there], far, preferred_element_type=F32)
            )

    for k in range(wide):
        start = pl.multiple_of((place ^ k) * rows, rows)
        outs[k][...] = held[pl.ds(start, rows), :].astype(BF16)


def grad_blocks(wide, mine, other, factor, far):
    rows, width = mine.shape
    half = factor.shape[1]
    vmem = pl.BlockSpec(memory_space=pltpu.VMEM)
    return pl.pallas_call(
        functools.partial(grad_kernel, wide),
        out_shape=[jax.ShapeDtypeStruct((rows // wide, half), BF16)] * wide,
        in_specs=[vmem] * 4,
        out_specs=[vmem] * wide,
        scratch_shapes=[pltpu.VMEM((rows, half), F32)],
        compiler_params=pltpu.CompilerParams(vmem_limit_bytes=8 << 20),
        cost_estimate=pl.CostEstimate(
            flops=4 * rows * width * half, bytes_accessed=12 * rows * width, transcendentals=0
        ),
    )(mine, other, factor, far)


def fetch_kernel(first, queries_ref, out_ref, sem):
    copy = pltpu.make_async_copy(queries_ref.at[pl.ds(first, out_ref.shape[0])], out_ref, sem)
    copy.start()
    copy.wait()


def fetch(queries, first, count):
    return pl.pallas_call(
        functools.partial(fetch_kernel, first),
        out_shape=pltpu.VMEM((count,) + queries.shape[1:], BF16),
        in_specs=[pl.BlockSpec(memory_space=pltpu.HBM)],
        out_specs=pl.BlockSpec(memory_space=pltpu.VMEM),
        scratch_shapes=[pltpu.SemaphoreType.DMA],
        compiler_params=pltpu.CompilerParams(vmem_limit_bytes=2 << 20),
        cost_estimate=pl.CostEstimate(
            flops=0,
            bytes_accessed=2 * count * queries.shape[1] * queries.shape[2],
            transcendentals=0,
        ),
    )(pltpu.with_memory_space_constraint(queries, pltpu.HBM))


def tagged_fetch_kernel(first, wide, order_ref, queries_ref, out_ref, tags_ref, order, sems):
    order_copy = pltpu.make_async_copy(order_ref, order, sems.at[0])
    order_copy.start()
    copy = pltpu.make_async_copy(
        queries_ref.at[pl.ds(first, out_ref.shape[0])], out_ref, sems.at[1]
    )
    copy.start()
    order_copy.wait()
    row = lax.broadcasted_iota(jnp.int32, tags_ref.shape, 0)
    lane = lax.broadcasted_iota(jnp.int32, tags_ref.shape, 1)
    tags = jnp.zeros(tags_ref.shape, F32)
    for k in range(wide):
        goal = lax.axis_index("parts") * wide + order[lax.axis_index("wide") ^ k]
        tags += jnp.where((row == k) & (lane == goal), 1.0, 0.0)
    tags_ref[...] = tags.astype(BF16)
    copy.wait()


def tagged_fetch(wide, order, queries, first, count):
    width = queries.shape[2]
    vmem = pl.BlockSpec(memory_space=pltpu.VMEM)
    return pl.pallas_call(
        functools.partial(tagged_fetch_kernel, first, wide),
        out_shape=(
            pltpu.VMEM((count,) + queries.shape[1:], BF16),
            jax.ShapeDtypeStruct((GROUP, width), BF16),
        ),
        in_specs=[pl.BlockSpec(memory_space=pl.ANY), pl.BlockSpec(memory_space=pltpu.HBM)],
        out_specs=(vmem, vmem),
        scratch_shapes=[pltpu.SMEM(order.shape, jnp.int32), pltpu.SemaphoreType.DMA((2,))],
        compiler_params=pltpu.CompilerParams(vmem_limit_bytes=2 << 20),
        cost_estimate=pl.CostEstimate(
            flops=0, bytes_accessed=2 * count * queries.shape[1] * width, transcendentals=0
        ),
    )(order, pltpu.with_memory_space_constraint(queries, pltpu.HBM))


def exchange_kernel(wide, tags_ref, *refs):
    grads, out_ref = refs[:wide], refs[wide]
    rows = grads[0].shape[0]
    share = rows // lax.axis_size("parts")
    first = pl.multiple_of((1 - lax.axis_index("parts")) * share, share)
    for k in range(wide):
        out_ref[k * share : (k + 1) * share, :] = grads[k][pl.ds(first, share), :]
    out_ref[wide * share :, :] = tags_ref[...]


def exchange_block(parts, tags, grads):
    wide = len(grads)
    rows, width = grads[0].shape
    vmem = pl.BlockSpec(memory_space=pltpu.VMEM)
    return pl.pallas_call(
        functools.partial(exchange_kernel, wide),
        out_shape=jax.ShapeDtypeStruct((wide * rows // parts + GROUP, width), BF16),
        in_specs=[vmem] * (wide + 1),
        out_specs=vmem,
        compiler_params=pltpu.CompilerParams(vmem_limit_bytes=2 << 20),
        cost_estimate=pl.CostEstimate(
            flops=0, bytes_accessed=4 * wide * rows * width, transcendentals=0
        ),
    )(tags, *grads)


def joined_rows(source, first, count, start, rows):
    width = source.shape[2]
    return jnp.concatenate(
        [
            source[pl.ds(first, count), pl.ds(start + g, GROUP), :].reshape(count * GROUP, width)
            for g in range(0, rows, GROUP)
        ],
        axis=1,
    )


def group_sums(lines, weights, count):
    lanes = weights.shape[0]
    lane = lax.broadcasted_iota(jnp.int32, (GROUP, lanes), 1)
    diagonal = lax.broadcasted_iota(jnp.int32, (GROUP, lanes), 0) == lane % GROUP
    found = lax.dot_general(lines, weights, NT, preferred_element_type=F32)
    return jnp.sum(jnp.where(diagonal, found.reshape(count, GROUP, lanes), 0.0), axis=1)


def add_up(place, sums):
    high = sums.astype(BF16)
    low = (sums - high.astype(F32)).astype(BF16)
    return lax.dot_general(place, high, NT, preferred_element_type=F32) + lax.dot_general(
        place, low, NT, preferred_element_type=F32
    )


def place_of(block_ref, lanes, first):
    tags = block_ref[block_ref.shape[0] - GROUP :, :]
    source = lax.broadcasted_iota(jnp.int32, (GROUP, lanes), 1) // GROUP - first
    owner = source == lax.broadcasted_iota(jnp.int32, (GROUP, lanes), 0)
    return lax.dot_general(
        tags, owner.astype(F32).astype(BF16), TN, preferred_element_type=F32
    )[:GROUP]


LOOPS = 2


def local_score_kernel(wide, sets, tags_ref, *refs):
    grads, refs = refs[:wide], refs[wide:]
    here, (queries_ref, out_ref, held_ref, sums, sems) = refs[:sets], refs[sets:]
    rows, width = grads[0].shape
    part, parts = lax.axis_index("parts"), lax.axis_size("parts")
    share = rows // parts
    done = sum(source.shape[0] for source in here)
    half = held_ref.shape[0] // 2
    own = pl.multiple_of(part * share, share)

    def copy(i):
        return pltpu.make_async_copy(
            queries_ref.at[pl.ds(done + i * half, half), pl.ds(own, share), :],
            held_ref.at[pl.ds(i * half, half)],
            sems.at[i],
        )

    for i in range(2):
        copy(i).start()
    weights = jnp.concatenate(
        [
            jnp.concatenate([grad[g : g + GROUP, :] for grad in grads], axis=0)
            for g in range(0, rows, GROUP)
        ],
        axis=1,
    )
    def step(i, carry):
        counts = [source.shape[0] // LOOPS for source in here]
        lines = [
            joined_rows(source, pl.multiple_of(i * count, 8), count, 0, rows)
            for source, count in zip(here, counts)
        ]
        found = group_sums(jnp.concatenate(lines, axis=0), weights, sum(counts))
        at, taken = 0, 0
        for count in counts:
            to = pl.multiple_of(at + i * count, 8)
            sums[pl.ds(to, count), :] = found[taken : taken + count]
            at, taken = at + count * LOOPS, taken + count
        return carry

    lax.fori_loop(0, LOOPS, step, 0)
    out_ref[...] = add_up(place_of(tags_ref, wide * GROUP, 0).astype(BF16), sums[...])

    def finish(i, carry):
        copy(i).wait()
        return carry

    lax.fori_loop(0, 2, finish, 0)


def local_scores(parts, tagged, grads, here, queries, count):
    wide = len(grads)
    rows, width = grads[0].shape
    done = sum(x.shape[0] for x in here)
    vmem = pl.BlockSpec(memory_space=pltpu.VMEM)
    return pl.pallas_call(
        functools.partial(local_score_kernel, wide, len(here)),
        out_shape=(
            jax.ShapeDtypeStruct((GROUP, done), F32),
            pltpu.VMEM((count, rows // parts, width), BF16),
        ),
        in_specs=[vmem] * (1 + wide + len(here))
        + [pl.BlockSpec(memory_space=pltpu.HBM)],
        out_specs=(vmem, vmem),
        scratch_shapes=[
            pltpu.VMEM((done, wide * GROUP), F32),
            pltpu.SemaphoreType.DMA((2,)),
        ],
        compiler_params=pltpu.CompilerParams(vmem_limit_bytes=10 << 20),
        cost_estimate=pl.CostEstimate(
            flops=2 * done * rows * width * 128,
            bytes_accessed=2 * (done + count) * rows * width,
            transcendentals=0,
        ),
    )(
        tagged,
        *grads,
        *(pltpu.with_memory_space_constraint(x, pltpu.VMEM) for x in here),
        pltpu.with_memory_space_constraint(queries, pltpu.HBM),
    )


def shared_score_kernel(wide, pieces, tags_ref, *refs):
    grads, refs = refs[:wide], refs[wide:]
    far_ref, local_ref, here_ref, queries_ref, out_ref, held, sums, sems = refs
    rows, width = grads[0].shape
    part, parts = lax.axis_index("parts"), lax.axis_size("parts")
    share = rows // parts
    local = local_ref.shape[1]
    ready = here_ref.shape[0]
    piece = held.shape[0] // pieces
    own = pl.multiple_of(part * share, share)

    def copy(i):
        return pltpu.make_async_copy(
            queries_ref.at[pl.ds(local + ready + i * piece, piece), pl.ds(own, share), :],
            held.at[pl.ds(i * piece, piece)],
            sems.at[i],
        )

    depth = min(2, pieces)
    for i in range(depth):
        copy(i).start()
    lanes = parts * wide * GROUP
    weights = jnp.concatenate(
        [
            jnp.concatenate(
                [grad[pl.ds(own + g, GROUP), :] for grad in grads]
                + [far_ref[k * share + g : k * share + g + GROUP, :] for k in range(wide)],
                axis=0,
            )
            for g in range(0, share, GROUP)
        ],
        axis=1,
    )

    def ready_step(i, carry):
        at = pl.multiple_of(i * piece, GROUP)
        lines = joined_rows(here_ref, at, piece, 0, share)
        sums[pl.ds(local + at, piece), :] = group_sums(lines, weights, piece)
        return carry

    lax.fori_loop(0, ready // piece, ready_step, 0)

    def late_step(i, carry):
        copy(i).wait()

        @pl.when(i + depth < pieces)
        def _():
            copy(i + depth).start()

        at = pl.multiple_of(i * piece, GROUP)
        lines = joined_rows(held, at, piece, 0, share)
        sums[pl.ds(local + ready + at, piece), :] = group_sums(lines, weights, piece)
        return carry

    lax.fori_loop(0, pieces, late_step, 0)

    place = (place_of(tags_ref, lanes, 0) + place_of(far_ref, lanes, wide)).astype(BF16)
    span = out_ref.shape[2]
    blocks = queries_ref.shape[0] // span
    for b in range(blocks):
        if (b + 1) * span <= local:
            for m in range(parts * wide):
                out_ref[m * blocks + b] = local_ref[m : m + 1, b * span : (b + 1) * span]
        else:
            scores = add_up(place, sums[b * span : (b + 1) * span, :])
            for m in range(parts * wide):
                out_ref[m * blocks + b] = scores[m : m + 1]


def shared_scores(parts, blocks, pieces, tagged, grads, far, local, here, queries):
    wide = len(grads)
    rows, width = grads[0].shape
    total = queries.shape[0]
    late = total - local.shape[1] - here.shape[0]
    vmem = pl.BlockSpec(memory_space=pltpu.VMEM)
    return pl.pallas_call(
        functools.partial(shared_score_kernel, wide, pieces),
        out_shape=jax.ShapeDtypeStruct((parts * wide * blocks, 1, total // blocks), F32),
        in_specs=[vmem] * (wide + 4)
        + [pl.BlockSpec(memory_space=pltpu.HBM)],
        out_specs=vmem,
        scratch_shapes=[
            pltpu.VMEM((late, rows // parts, width), BF16),
            pltpu.VMEM((total, parts * wide * GROUP), F32),
            pltpu.SemaphoreType.DMA((pieces,)),
        ],
        compiler_params=pltpu.CompilerParams(vmem_limit_bytes=20 << 20),
        cost_estimate=pl.CostEstimate(
            flops=2 * total * rows * width * 128,
            bytes_accessed=2 * late * rows * width,
            transcendentals=0,
        ),
    )(
        tagged,
        *grads,
        far,
        local,
        pltpu.with_memory_space_constraint(here, pltpu.VMEM),
        pltpu.with_memory_space_constraint(queries, pltpu.HBM),
    )


def shared(activations, deltas, act_factor, delta_factor, queries, assignment, padding):
    parts, wide, rep, sub = (lax.axis_size(a) for a in ("parts", "wide", "rep", "sub"))
    half = act_factor.shape[1]
    early = queries.shape[0] // 8
    later = 3 * early
    own_block = lax.dynamic_slice_in_dim(act_factor, lax.axis_index("rep") * half, half, axis=0)
    far_block = lax.ppermute(own_block, "rep", [(0, 1), (1, 0)])
    mine, columns, first = row_product(
        padding, deltas[0], activations[0], delta_factor, act_factor, queries, early
    )
    second = fetch(queries, early, early // 2)
    third, tags = tagged_fetch(wide, assignment, queries, 3 * early // 2, early // 2)
    mine, columns, far_block = lax.optimization_barrier((mine, columns, far_block))
    other = lax.ppermute(mine, "sub", [(0, 1), (1, 0)])
    other, second = lax.optimization_barrier((other, second))
    sent = grad_blocks(wide, mine, other, columns, far_block)
    grads = [sent[0]] + [
        lax.ppermute(sent[k], "wide", [(i, i ^ k) for i in range(wide)]) for k in range(1, wide)
    ]
    tagged = exchange_block(parts, tags, grads)
    far = lax.ppermute(tagged, "parts", [(0, 1), (1, 0)])
    local, held = local_scores(
        parts, tagged, grads, [first, second, third], queries, later
    )
    partial = shared_scores(
        parts, rep * sub, 2, tagged, grads, far, local, held, queries
    )
    gathered = lax.all_to_all(
        partial, ("parts", "wide", "rep", "sub"), split_axis=0, concat_axis=0, tiled=True
    )
    return jnp.sum(gathered, axis=0)


def general(activations, deltas, act_factor, delta_factor, queries, assignment, padding):
    seq_dev, tok_dev, _ = activations.shape
    full_length = tok_dev * lax.axis_size("sub")
    token_start = lax.axis_index("sub") * tok_dev
    positions = token_start + lax.broadcasted_iota(jnp.int32, (seq_dev, tok_dev), 1)
    kept_mask = positions < (full_length - padding)[:, None]
    masked = jnp.where(kept_mask[:, :, None], deltas, jnp.zeros((), BF16))
    delta_proj = jnp.einsum(
        "stw,wi->sti", masked, delta_factor, preferred_element_type=F32
    ).astype(BF16)
    act_proj = jnp.einsum(
        "stw,wj->stj",
        activations,
        lax.all_gather(act_factor, "rep", axis=1, tiled=True),
        preferred_element_type=F32,
    ).astype(BF16)
    partial_value = jnp.einsum("sti,stj->sij", delta_proj, act_proj, preferred_element_type=F32)
    summed = lax.psum_scatter(partial_value, "sub", scatter_dimension=2, tiled=True).astype(BF16)
    regrouped = lax.all_to_all(summed, "wide", split_axis=1, concat_axis=0, tiled=True)
    seq_total = regrouped.shape[0]
    grad_rows = regrouped.reshape(seq_total, -1)
    query_rows = queries.reshape(queries.shape[0], -1)
    partial_scores = lax.dot_general(grad_rows, query_rows, NT, preferred_element_type=F32)
    inverse_order = (
        jnp.zeros((seq_total,), jnp.int32)
        .at[assignment]
        .set(jnp.arange(seq_total, dtype=jnp.int32))
    )
    ranked = jnp.take(partial_scores, inverse_order, axis=0)
    by_column = lax.psum_scatter(ranked, ("rep", "sub"), scatter_dimension=1, tiled=True)
    return lax.psum_scatter(by_column, "wide", scatter_dimension=0, tiled=True)


def shards(activations, deltas, act_factor, delta_factor, queries, assignment, padding):
    parts, wide, rep, sub = (lax.axis_size(a) for a in ("parts", "wide", "rep", "sub"))
    fits = (
        parts == 2
        and rep == 2
        and sub == 2
        and wide in (2, 4)
        and activations.shape[0] == 1
        and queries.shape[1] % (parts * GROUP) == 0
        and queries.shape[0] % (16 * GROUP) == 0
        and act_factor.shape[1] % 128 == 0
    )
    body = shared if fits else general
    return body(activations, deltas, act_factor, delta_factor, queries, assignment, padding)


def solution(mesh):
    placed = (
        P(("parts", "wide"), "sub", None),
        P(("parts", "wide"), "sub", None),
        P(None, "rep"),
        P(None, "rep"),
        P(None, ("rep", "wide"), "sub"),
        P("parts"),
        P(("parts", "wide")),
    )
    return jax.shard_map(
        shards,
        mesh=mesh,
        in_specs=placed,
        out_specs=P(("parts", "wide"), ("rep", "sub")),
        check_vma=False,
    )
```

```python
import functools

import jax
import jax.numpy as jnp
from jax import lax
from jax.experimental import pallas as pl
from jax.experimental.pallas import tpu as pltpu
from jax.sharding import PartitionSpec as P

GROUP = 16
F32 = jnp.float32
BF16 = jnp.bfloat16
NT = (((1,), (1,)), ((), ()))
TN = (((0,), (0,)), ((), ()))


def row_product_kernel(
    pad_ref, deltas_ref, acts_ref, row_factor_ref, col_factor_ref, queries_ref,
    out_ref, sent_ref, col_out_ref, early_ref,
    pad_in, deltas_in, acts_in, factor_in, sems,
):
    steps, tokens, _ = deltas_in.shape
    first = lax.axis_index("sub") * steps * tokens

    def copy(source, held, which, i):
        return pltpu.make_async_copy(
            source.at[pl.ds(i * tokens, tokens), :], held.at[i], sems.at[which, i]
        )

    row_copy = pltpu.make_async_copy(row_factor_ref, factor_in, sems.at[2, 0])
    col_copy = pltpu.make_async_copy(col_factor_ref, col_out_ref, sems.at[2, 1])
    pad_copy = pltpu.make_async_copy(pad_ref, pad_in, sems.at[2, 2])
    pad_copy.start()
    row_copy.start()
    for i in range(steps):
        copy(deltas_ref, deltas_in, 0, i).start()
        copy(acts_ref, acts_in, 1, i).start()
    col_copy.start()
    early_copy = pltpu.make_async_copy(
        queries_ref.at[pl.ds(0, early_ref.shape[0])], early_ref, sems.at[2, 3]
    )
    early_copy.start()
    out_ref[...] = jnp.zeros(out_ref.shape, F32)
    pad_copy.wait()
    row_copy.wait()
    limit = lax.axis_size("sub") * steps * tokens - pad_in[0]

    def step(i, carry):
        copy(deltas_ref, deltas_in, 0, i).wait()
        copy(acts_ref, acts_in, 1, i).wait()
        position = first + i * tokens + lax.broadcasted_iota(jnp.int32, (tokens, 1), 0)
        masked = jnp.where(position < limit, deltas_in[i], jnp.zeros((), BF16))
        proj = jnp.dot(masked, factor_in[...], preferred_element_type=F32).astype(BF16)
        out_ref[...] += lax.dot_general(proj, acts_in[i], TN, preferred_element_type=F32)
        return carry

    lax.fori_loop(0, steps, step, 0)
    sent_ref[...] = out_ref[...].astype(BF16)
    col_copy.wait()
    early_copy.wait()


def row_product(padding, deltas, acts, row_factor, col_factor, queries, early):
    tokens, width = deltas.shape
    rows = row_factor.shape[1]
    steps = max(1, tokens // 512)
    hbm = pl.BlockSpec(memory_space=pltpu.HBM)
    vmem = pl.BlockSpec(memory_space=pltpu.VMEM)
    operands = [padding] + [
        pltpu.with_memory_space_constraint(x, pltpu.HBM)
        for x in (deltas, acts, row_factor, col_factor, queries)
    ]
    return pl.pallas_call(
        row_product_kernel,
        out_shape=(
            jax.ShapeDtypeStruct((rows, width), F32),
            jax.ShapeDtypeStruct((rows, width), BF16),
            jax.ShapeDtypeStruct(col_factor.shape, BF16),
            pltpu.VMEM((early,) + queries.shape[1:], BF16),
        ),
        in_specs=[pl.BlockSpec(memory_space=pl.ANY)] + [hbm] * 5,
        out_specs=(vmem, vmem, vmem, vmem),
        scratch_shapes=[
            pltpu.SMEM(padding.shape, jnp.int32),
            pltpu.VMEM((steps, tokens // steps, width), BF16),
            pltpu.VMEM((steps, tokens // steps, width), BF16),
            pltpu.VMEM(row_factor.shape, BF16),
            pltpu.SemaphoreType.DMA((3, max(4, steps))),
        ],
        compiler_params=pltpu.CompilerParams(vmem_limit_bytes=12 << 20),
        cost_estimate=pl.CostEstimate(
            flops=4 * tokens * width * rows, bytes_accessed=4 * tokens * width, transcendentals=0
        ),
    )(*operands)


def grad_kernel(wide, mine_ref, other_ref, factor_ref, far_ref, *outs_and_scratch):
    *outs, held = outs_and_scratch
    rep, sub, place = (lax.axis_index(a) for a in ("rep", "sub", "wide"))
    half = factor_ref.shape[1]
    rows = mine_ref.shape[0] // wide
    summed = mine_ref[...] + other_ref[...].astype(F32)
    high = summed.astype(BF16)
    low = (summed - high.astype(F32)).astype(BF16)

    @pl.when(rep == sub)
    def _():
        whole = factor_ref[...]
        held[...] = jnp.dot(high, whole, preferred_element_type=F32) + jnp.dot(
            low, whole, preferred_element_type=F32
        )

    for index in range(2):

        @pl.when((rep != sub) & (rep == index))
        def _():
            here = slice(index * half, (index + 1) * half)
            there = slice((1 - index) * half, (2 - index) * half)
            near, far = factor_ref[there, :], far_ref[...]
            held[...] = (
                lax.dot_general(high[:, here], near, NT, preferred_element_type=F32)
                + lax.dot_general(low[:, here], near, NT, preferred_element_type=F32)
                + jnp.dot(high[:, there], far, preferred_element_type=F32)
                + jnp.dot(low[:, there], far, preferred_element_type=F32)
            )

    for k in range(wide):
        start = pl.multiple_of((place ^ k) * rows, rows)
        outs[k][...] = held[pl.ds(start, rows), :].astype(BF16)


def grad_blocks(wide, mine, other, factor, far):
    rows, width = mine.shape
    half = factor.shape[1]
    vmem = pl.BlockSpec(memory_space=pltpu.VMEM)
    return pl.pallas_call(
        functools.partial(grad_kernel, wide),
        out_shape=[jax.ShapeDtypeStruct((rows // wide, half), BF16)] * wide,
        in_specs=[vmem] * 4,
        out_specs=[vmem] * wide,
        scratch_shapes=[pltpu.VMEM((rows, half), F32)],
        compiler_params=pltpu.CompilerParams(vmem_limit_bytes=8 << 20),
        cost_estimate=pl.CostEstimate(
            flops=4 * rows * width * half, bytes_accessed=12 * rows * width, transcendentals=0
        ),
    )(mine, other, factor, far)


def fetch_kernel(first, queries_ref, out_ref, sem):
    copy = pltpu.make_async_copy(queries_ref.at[pl.ds(first, out_ref.shape[0])], out_ref, sem)
    copy.start()
    copy.wait()


def fetch(queries, first, count):
    return pl.pallas_call(
        functools.partial(fetch_kernel, first),
        out_shape=pltpu.VMEM((count,) + queries.shape[1:], BF16),
        in_specs=[pl.BlockSpec(memory_space=pltpu.HBM)],
        out_specs=pl.BlockSpec(memory_space=pltpu.VMEM),
        scratch_shapes=[pltpu.SemaphoreType.DMA],
        compiler_params=pltpu.CompilerParams(vmem_limit_bytes=2 << 20),
        cost_estimate=pl.CostEstimate(
            flops=0,
            bytes_accessed=2 * count * queries.shape[1] * queries.shape[2],
            transcendentals=0,
        ),
    )(pltpu.with_memory_space_constraint(queries, pltpu.HBM))


def tagged_fetch_kernel(first, wide, order_ref, queries_ref, out_ref, tags_ref, order, sems):
    order_copy = pltpu.make_async_copy(order_ref, order, sems.at[0])
    order_copy.start()
    copy = pltpu.make_async_copy(
        queries_ref.at[pl.ds(first, out_ref.shape[0])], out_ref, sems.at[1]
    )
    copy.start()
    order_copy.wait()
    row = lax.broadcasted_iota(jnp.int32, tags_ref.shape, 0)
    lane = lax.broadcasted_iota(jnp.int32, tags_ref.shape, 1)
    tags = jnp.zeros(tags_ref.shape, F32)
    for k in range(wide):
        goal = lax.axis_index("parts") * wide + order[lax.axis_index("wide") ^ k]
        tags += jnp.where((row == k) & (lane == goal), 1.0, 0.0)
    tags_ref[...] = tags.astype(BF16)
    copy.wait()


def tagged_fetch(wide, order, queries, first, count):
    width = queries.shape[2]
    vmem = pl.BlockSpec(memory_space=pltpu.VMEM)
    return pl.pallas_call(
        functools.partial(tagged_fetch_kernel, first, wide),
        out_shape=(
            pltpu.VMEM((count,) + queries.shape[1:], BF16),
            jax.ShapeDtypeStruct((GROUP, width), BF16),
        ),
        in_specs=[pl.BlockSpec(memory_space=pl.ANY), pl.BlockSpec(memory_space=pltpu.HBM)],
        out_specs=(vmem, vmem),
        scratch_shapes=[pltpu.SMEM(order.shape, jnp.int32), pltpu.SemaphoreType.DMA((2,))],
        compiler_params=pltpu.CompilerParams(vmem_limit_bytes=2 << 20),
        cost_estimate=pl.CostEstimate(
            flops=0, bytes_accessed=2 * count * queries.shape[1] * width, transcendentals=0
        ),
    )(order, pltpu.with_memory_space_constraint(queries, pltpu.HBM))


def exchange_kernel(wide, tags_ref, *refs):
    grads, out_ref = refs[:wide], refs[wide]
    rows = grads[0].shape[0]
    share = rows // lax.axis_size("parts")
    first = pl.multiple_of((1 - lax.axis_index("parts")) * share, share)
    for k in range(wide):
        out_ref[k * share : (k + 1) * share, :] = grads[k][pl.ds(first, share), :]
    out_ref[wide * share :, :] = tags_ref[...]


def exchange_block(parts, tags, grads):
    wide = len(grads)
    rows, width = grads[0].shape
    vmem = pl.BlockSpec(memory_space=pltpu.VMEM)
    return pl.pallas_call(
        functools.partial(exchange_kernel, wide),
        out_shape=jax.ShapeDtypeStruct((wide * rows // parts + GROUP, width), BF16),
        in_specs=[vmem] * (wide + 1),
        out_specs=vmem,
        compiler_params=pltpu.CompilerParams(vmem_limit_bytes=2 << 20),
        cost_estimate=pl.CostEstimate(
            flops=0, bytes_accessed=4 * wide * rows * width, transcendentals=0
        ),
    )(tags, *grads)


def joined_rows(source, first, count, start, rows):
    width = source.shape[2]
    return jnp.concatenate(
        [
            source[pl.ds(first, count), pl.ds(start + g, GROUP), :].reshape(count * GROUP, width)
            for g in range(0, rows, GROUP)
        ],
        axis=1,
    )


def group_sums(lines, weights, count):
    lanes = weights.shape[0]
    lane = lax.broadcasted_iota(jnp.int32, (GROUP, lanes), 1)
    diagonal = lax.broadcasted_iota(jnp.int32, (GROUP, lanes), 0) == lane % GROUP
    found = lax.dot_general(lines, weights, NT, preferred_element_type=F32)
    return jnp.sum(jnp.where(diagonal, found.reshape(count, GROUP, lanes), 0.0), axis=1)


def add_up(place, sums):
    high = sums.astype(BF16)
    low = (sums - high.astype(F32)).astype(BF16)
    return lax.dot_general(place, high, NT, preferred_element_type=F32) + lax.dot_general(
        place, low, NT, preferred_element_type=F32
    )


def place_of(block_ref, lanes, first):
    tags = block_ref[block_ref.shape[0] - GROUP :, :]
    source = lax.broadcasted_iota(jnp.int32, (GROUP, lanes), 1) // GROUP - first
    owner = source == lax.broadcasted_iota(jnp.int32, (GROUP, lanes), 0)
    return lax.dot_general(
        tags, owner.astype(F32).astype(BF16), TN, preferred_element_type=F32
    )[:GROUP]


LOOPS = 2


def local_score_kernel(wide, sets, tags_ref, *refs):
    grads, refs = refs[:wide], refs[wide:]
    here, (queries_ref, out_ref, held_ref, sums, sems) = refs[:sets], refs[sets:]
    rows, width = grads[0].shape
    part, parts = lax.axis_index("parts"), lax.axis_size("parts")
    share = rows // parts
    done = sum(source.shape[0] for source in here)
    half = held_ref.shape[0] // 2
    own = pl.multiple_of(part * share, share)

    def copy(i):
        return pltpu.make_async_copy(
            queries_ref.at[pl.ds(done + i * half, half), pl.ds(own, share), :],
            held_ref.at[pl.ds(i * half, half)],
            sems.at[i],
        )

    for i in range(2):
        copy(i).start()
    weights = jnp.concatenate(
        [
            jnp.concatenate([grad[g : g + GROUP, :] for grad in grads], axis=0)
            for g in range(0, rows, GROUP)
        ],
        axis=1,
    )
    def step(i, carry):
        counts = [source.shape[0] // LOOPS for source in here]
        lines = [
            joined_rows(source, pl.multiple_of(i * count, 8), count, 0, rows)
            for source, count in zip(here, counts)
        ]
        found = group_sums(jnp.concatenate(lines, axis=0), weights, sum(counts))
        at, taken = 0, 0
        for count in counts:
            to = pl.multiple_of(at + i * count, 8)
            sums[pl.ds(to, count), :] = found[taken : taken + count]
            at, taken = at + count * LOOPS, taken + count
        return carry

    lax.fori_loop(0, LOOPS, step, 0)
    out_ref[...] = add_up(place_of(tags_ref, wide * GROUP, 0).astype(BF16), sums[...])

    def finish(i, carry):
        copy(i).wait()
        return carry

    lax.fori_loop(0, 2, finish, 0)


def local_scores(parts, tagged, grads, here, queries, count):
    wide = len(grads)
    rows, width = grads[0].shape
    done = sum(x.shape[0] for x in here)
    vmem = pl.BlockSpec(memory_space=pltpu.VMEM)
    return pl.pallas_call(
        functools.partial(local_score_kernel, wide, len(here)),
        out_shape=(
            jax.ShapeDtypeStruct((GROUP, done), F32),
            pltpu.VMEM((count, rows // parts, width), BF16),
        ),
        in_specs=[vmem] * (1 + wide + len(here))
        + [pl.BlockSpec(memory_space=pltpu.HBM)],
        out_specs=(vmem, vmem),
        scratch_shapes=[
            pltpu.VMEM((done, wide * GROUP), F32),
            pltpu.SemaphoreType.DMA((2,)),
        ],
        compiler_params=pltpu.CompilerParams(vmem_limit_bytes=10 << 20),
        cost_estimate=pl.CostEstimate(
            flops=2 * done * rows * width * 128,
            bytes_accessed=2 * (done + count) * rows * width,
            transcendentals=0,
        ),
    )(
        tagged,
        *grads,
        *(pltpu.with_memory_space_constraint(x, pltpu.VMEM) for x in here),
        pltpu.with_memory_space_constraint(queries, pltpu.HBM),
    )


def shared_score_kernel(wide, pieces, tags_ref, *refs):
    grads, refs = refs[:wide], refs[wide:]
    far_ref, local_ref, here_ref, queries_ref, out_ref, held, sums, sems = refs
    rows, width = grads[0].shape
    part, parts = lax.axis_index("parts"), lax.axis_size("parts")
    share = rows // parts
    local = local_ref.shape[1]
    ready = here_ref.shape[0]
    piece = held.shape[0] // pieces
    own = pl.multiple_of(part * share, share)

    def copy(i):
        return pltpu.make_async_copy(
            queries_ref.at[pl.ds(local + ready + i * piece, piece), pl.ds(own, share), :],
            held.at[pl.ds(i * piece, piece)],
            sems.at[i],
        )

    depth = min(2, pieces)
    for i in range(depth):
        copy(i).start()
    lanes = parts * wide * GROUP
    weights = jnp.concatenate(
        [
            jnp.concatenate(
                [grad[pl.ds(own + g, GROUP), :] for grad in grads]
                + [far_ref[k * share + g : k * share + g + GROUP, :] for k in range(wide)],
                axis=0,
            )
            for g in range(0, share, GROUP)
        ],
        axis=1,
    )

    def ready_step(i, carry):
        at = pl.multiple_of(i * piece, GROUP)
        lines = joined_rows(here_ref, at, piece, 0, share)
        sums[pl.ds(local + at, piece), :] = group_sums(lines, weights, piece)
        return carry

    lax.fori_loop(0, ready // piece, ready_step, 0)

    def late_step(i, carry):
        copy(i).wait()

        @pl.when(i + depth < pieces)
        def _():
            copy(i + depth).start()

        at = pl.multiple_of(i * piece, GROUP)
        lines = joined_rows(held, at, piece, 0, share)
        sums[pl.ds(local + ready + at, piece), :] = group_sums(lines, weights, piece)
        return carry

    lax.fori_loop(0, pieces, late_step, 0)

    place = (place_of(tags_ref, lanes, 0) + place_of(far_ref, lanes, wide)).astype(BF16)
    span = out_ref.shape[2]
    blocks = queries_ref.shape[0] // span
    for b in range(blocks):
        if (b + 1) * span <= local:
            for m in range(parts * wide):
                out_ref[m * blocks + b] = local_ref[m : m + 1, b * span : (b + 1) * span]
        else:
            scores = add_up(place, sums[b * span : (b + 1) * span, :])
            for m in range(parts * wide):
                out_ref[m * blocks + b] = scores[m : m + 1]


def shared_scores(parts, blocks, pieces, tagged, grads, far, local, here, queries):
    wide = len(grads)
    rows, width = grads[0].shape
    total = queries.shape[0]
    late = total - local.shape[1] - here.shape[0]
    vmem = pl.BlockSpec(memory_space=pltpu.VMEM)
    return pl.pallas_call(
        functools.partial(shared_score_kernel, wide, pieces),
        out_shape=jax.ShapeDtypeStruct((parts * wide * blocks, 1, total // blocks), F32),
        in_specs=[vmem] * (wide + 4)
        + [pl.BlockSpec(memory_space=pltpu.HBM)],
        out_specs=vmem,
        scratch_shapes=[
            pltpu.VMEM((late, rows // parts, width), BF16),
            pltpu.VMEM((total, parts * wide * GROUP), F32),
            pltpu.SemaphoreType.DMA((pieces,)),
        ],
        compiler_params=pltpu.CompilerParams(vmem_limit_bytes=20 << 20),
        cost_estimate=pl.CostEstimate(
            flops=2 * total * rows * width * 128,
            bytes_accessed=2 * late * rows * width,
            transcendentals=0,
        ),
    )(
        tagged,
        *grads,
        far,
        local,
        pltpu.with_memory_space_constraint(here, pltpu.VMEM),
        pltpu.with_memory_space_constraint(queries, pltpu.HBM),
    )


def shared(activations, deltas, act_factor, delta_factor, queries, assignment, padding):
    parts, wide, rep, sub = (lax.axis_size(a) for a in ("parts", "wide", "rep", "sub"))
    half = act_factor.shape[1]
    early = queries.shape[0] // 8
    later = 3 * early
    own_block = lax.dynamic_slice_in_dim(act_factor, lax.axis_index("rep") * half, half, axis=0)
    far_block = lax.ppermute(own_block, "rep", [(0, 1), (1, 0)])
    mine, rounded, columns, first = row_product(
        padding, deltas[0], activations[0], delta_factor, act_factor, queries, early
    )
    second = fetch(queries, early, 32)
    third, tags = tagged_fetch(wide, assignment, queries, early + 32, 128)
    rounded, columns, far_block = lax.optimization_barrier((rounded, columns, far_block))
    other = lax.ppermute(rounded, "sub", [(0, 1), (1, 0)])
    other, second = lax.optimization_barrier((other, second))
    sent = grad_blocks(wide, mine, other, columns, far_block)
    grads = [sent[0]] + [
        lax.ppermute(sent[k], "wide", [(i, i ^ k) for i in range(wide)]) for k in range(1, wide)
    ]
    tagged = exchange_block(parts, tags, grads)
    far = lax.ppermute(tagged, "parts", [(0, 1), (1, 0)])
    local, held = local_scores(
        parts, tagged, grads, [first, second, third], queries, later
    )
    partial = shared_scores(
        parts, rep * sub, 2, tagged, grads, far, local, held, queries
    )
    gathered = lax.all_to_all(
        partial, ("parts", "wide", "rep", "sub"), split_axis=0, concat_axis=0, tiled=True
    )
    return jnp.sum(gathered, axis=0)


def general(activations, deltas, act_factor, delta_factor, queries, assignment, padding):
    seq_dev, tok_dev, _ = activations.shape
    full_length = tok_dev * lax.axis_size("sub")
    token_start = lax.axis_index("sub") * tok_dev
    positions = token_start + lax.broadcasted_iota(jnp.int32, (seq_dev, tok_dev), 1)
    kept_mask = positions < (full_length - padding)[:, None]
    masked = jnp.where(kept_mask[:, :, None], deltas, jnp.zeros((), BF16))
    delta_proj = jnp.einsum(
        "stw,wi->sti", masked, delta_factor, preferred_element_type=F32
    ).astype(BF16)
    act_proj = jnp.einsum(
        "stw,wj->stj",
        activations,
        lax.all_gather(act_factor, "rep", axis=1, tiled=True),
        preferred_element_type=F32,
    ).astype(BF16)
    partial_value = jnp.einsum("sti,stj->sij", delta_proj, act_proj, preferred_element_type=F32)
    summed = lax.psum_scatter(partial_value, "sub", scatter_dimension=2, tiled=True).astype(BF16)
    regrouped = lax.all_to_all(summed, "wide", split_axis=1, concat_axis=0, tiled=True)
    seq_total = regrouped.shape[0]
    grad_rows = regrouped.reshape(seq_total, -1)
    query_rows = queries.reshape(queries.shape[0], -1)
    partial_scores = lax.dot_general(grad_rows, query_rows, NT, preferred_element_type=F32)
    inverse_order = (
        jnp.zeros((seq_total,), jnp.int32)
        .at[assignment]
        .set(jnp.arange(seq_total, dtype=jnp.int32))
    )
    ranked = jnp.take(partial_scores, inverse_order, axis=0)
    by_column = lax.psum_scatter(ranked, ("rep", "sub"), scatter_dimension=1, tiled=True)
    return lax.psum_scatter(by_column, "wide", scatter_dimension=0, tiled=True)


def shards(activations, deltas, act_factor, delta_factor, queries, assignment, padding):
    parts, wide, rep, sub = (lax.axis_size(a) for a in ("parts", "wide", "rep", "sub"))
    fits = (
        parts == 2
        and rep == 2
        and sub == 2
        and wide in (2, 4)
        and activations.shape[0] == 1
        and queries.shape[1] % (parts * GROUP) == 0
        and queries.shape[0] % (16 * GROUP) == 0
        and act_factor.shape[1] % 128 == 0
    )
    body = shared if fits else general
    return body(activations, deltas, act_factor, delta_factor, queries, assignment, padding)


def solution(mesh):
    placed = (
        P(("parts", "wide"), "sub", None),
        P(("parts", "wide"), "sub", None),
        P(None, "rep"),
        P(None, "rep"),
        P(None, ("rep", "wide"), "sub"),
        P("parts"),
        P(("parts", "wide")),
    )
    return jax.shard_map(
        shards,
        mesh=mesh,
        in_specs=placed,
        out_specs=P(("parts", "wide"), ("rep", "sub")),
        check_vma=False,
    )
```
